256 devices in a mesh: client: 32 (over x, z_lo, y), row: 8 (over z_hi, core).
Axes of the slice: x: 4, y: 4, z: 8 (z_hi: 4, z_lo: 2; z = z_hi * 2 + z_lo), core: 2. Of those that a mesh axis runs over, the one named last changes fastest.
Arguments:
- activations: bfloat16 [32, 4, 256, 5120], P('client', None, None, 'row'), may hold values from -6 to 6
- cotangent: bfloat16 [32, 4, 256, 27648], P('client', None, None, 'row'), may hold values from -6 to 6
- lengths: int32 [32, 4], P('client'), may hold values from 1 to 256, 768 in all within a row
- adapter_down: bfloat16 [32, 32, 5120], P('client', None, 'row'), may hold values from -6 to 6
- adapter_up: bfloat16 [32, 32, 27648], P('client', None, 'row'), may hold values from -6 to 6
Outputs:
- merged_down: bfloat16 [32, 5120], P(None, 'row')
- merged_up: bfloat16 [32, 27648], P(None, 'row')
The draws below stay inside these ranges and needn't reach their ends.
Inputs may be any that keep to these rules, and one draw needn't show every extreme that they name: For each client, its 4 lengths sum to 768, and one of them equals 256; the total holds for one client's row of lengths, not across clients.
All inputs are finite; a program needn't handle non-finite values.
Results may differ from the reference program's by a relative error of at most 0.0046.
Values may be sent and summed in bfloat16 or wider, within the bound.
A program may use at most 64 MiB of HBM per device.

```python
import math
import jax
import jax.numpy as jnp
import numpy as np
from jax import lax

D = 5120
FF = 27648
R = 32
SEQLEN = 256
SEQ = 4
CLIENTS = 32


def block_scale(key, dims, pieces, low, top_value):
    loudness, own = 1.0, jax.random.fold_in(key, 6)
    for axis_at, parts in pieces:
        draws = jnp.exp(jax.random.uniform(jax.random.fold_in(own, axis_at), (parts,), jnp.float32, low / len(pieces), top_value / len(pieces)))
        loudness = loudness * jnp.repeat(draws, dims[axis_at] // parts).reshape([-1 if axis == axis_at else 1 for axis in range(len(dims))])
    return loudness


def length_profile(amount, total, reach, lean):
    weights = [(1 << 20) // math.isqrt(standing ** lean) + 1 for standing in range(2, amount + 1)]
    surplus, given = total - reach - (amount - 1), [1] * (amount - 1)
    while surplus > 0:
        movable = [i for i in range(amount - 1) if given[i] < reach]
        mass, budget = sum([weights[i] for i in movable]), surplus
        for i in movable:
            addition = min(reach - given[i], max(1, budget * weights[i] // mass), surplus)
            given[i] = given[i] + addition
            surplus = surplus - addition
    return np.array([reach] + given)


def uneven_parts(rng, count, total, most, skew):
    if count == 2:
        one = jax.random.randint(rng, (), max(1, total - most), min(most, total - 1) + 1)
        return jnp.stack([one, total - one])
    sizes = jnp.asarray(length_profile(count, total, most, skew), jnp.int32)
    pairs = (count - 1) // 2
    source_of, sink = sizes[1:1 + 2 * pairs:2], sizes[2:2 + 2 * pairs:2]
    room = jnp.minimum(source_of - 1, most - sink)
    passed = jax.random.randint(jax.random.fold_in(rng, 1), (pairs,), 0, 1 << 20) % (room + 1)
    sizes = sizes.at[1:1 + 2 * pairs:2].set(source_of - passed).at[2:2 + 2 * pairs:2].set(sink + passed)
    return sizes[jax.random.permutation(jax.random.fold_in(rng, 2), count)]


def scatter_about(own_key, extent, scale, reach, cuts=(), kind=jnp.bfloat16):
    level = block_scale(own_key, extent, cuts, -0.22, 0.18) if cuts else 1.0
    values = jax.random.normal(own_key, extent, jnp.float32) * scale * level
    return jnp.minimum(jnp.maximum(values, -reach), reach).astype(kind)


def setup_inputs(seed: int = 0) -> dict:
    seeds = jax.random.split(jax.random.key(seed), 6)
    return {
        "activations": scatter_about(seeds[0], (CLIENTS, SEQ, SEQLEN, D), 1.0, 6.0, ((0, 32), (3, 8))),
        "cotangent": scatter_about(seeds[1], (CLIENTS, SEQ, SEQLEN, FF), 1.0, 6.0, ((0, 32), (3, 8))),
        "lengths": jax.vmap(lambda own: uneven_parts(own, SEQ, 3 * SEQ * SEQLEN // 4, SEQLEN, 0))(jax.random.split(seeds[2], CLIENTS)).reshape((CLIENTS, SEQ)).astype(jnp.int32),
        "adapter_down": scatter_about(seeds[3], (CLIENTS, R, D), 1.0, 6.0, ((0, 32), (2, 8))),
        "adapter_up": scatter_about(seeds[4], (CLIENTS, R, FF), 1.0, 6.0, ((0, 32), (2, 8))),
    }


EPS = 1e-6


def client_terms(activations, cotangent, lengths, adapter_down, adapter_up):
    flat_in = activations.reshape(-1, D)
    flat_out = cotangent.reshape(-1, FF)
    projected = jnp.dot(flat_in, adapter_down.T, preferred_element_type=jnp.float32).reshape(SEQ, SEQLEN, R)
    pulled = jnp.dot(flat_out, adapter_up.T, preferred_element_type=jnp.float32).reshape(SEQ, SEQLEN, R)
    positions = jnp.arange(SEQLEN, dtype=jnp.int32)
    valid = (positions[None, :] < lengths[:, None]).astype(jnp.float32)
    weights = valid / lengths.astype(jnp.float32)[:, None]
    proj_w = (projected * weights[:, :, None]).astype(jnp.bfloat16)
    pull_w = (pulled * weights[:, :, None]).astype(jnp.bfloat16)
    grad_up = jnp.einsum("etr,etf->erf", proj_w.astype(jnp.float32), cotangent.astype(jnp.float32))
    grad_down = jnp.einsum("etr,etd->erd", pull_w.astype(jnp.float32), activations.astype(jnp.float32))
    fisher_up = jnp.sum(grad_up * grad_up, axis=0)
    fisher_down = jnp.sum(grad_down * grad_down, axis=0)
    return (fisher_down * adapter_down.astype(jnp.float32), fisher_down,
            fisher_up * adapter_up.astype(jnp.float32), fisher_up)


def reference(activations, cotangent, lengths, adapter_down, adapter_up):
    def accumulate(carry, inputs):
        terms = client_terms(*inputs)
        return tuple(a + b for a, b in zip(carry, terms)), None

    start = (jnp.zeros((R, D), jnp.float32), jnp.zeros((R, D), jnp.float32),
             jnp.zeros((R, FF), jnp.float32), jnp.zeros((R, FF), jnp.float32))
    totals, _ = lax.scan(accumulate, start, (activations, cotangent, lengths, adapter_down, adapter_up))
    merged_down = (totals[0] / (totals[1] + EPS)).astype(jnp.bfloat16)
    merged_up = (totals[2] / (totals[3] + EPS)).astype(jnp.bfloat16)
    return merged_down, merged_up
```

```python
import functools

import jax
import jax.numpy as jnp
from jax import lax
from jax.experimental import pallas as pl
from jax.experimental.pallas import tpu as pltpu
from jax.sharding import PartitionSpec as P

EPS = 1e-06
MESH = pl.DeviceIdType.MESH
LANES = 128
F32 = jnp.float32
BF16 = jnp.bfloat16
PART = F32
NT = (((1,), (1,)), ((), ()))


def kernel(
    nc, nr, act, cot, lens, down, up, out,
    data, adapt, lens_s, part, arrived, mine, tokens, terms, received, merged, gathered,
    load_sem, small_sem, rs_send, rs_recv, ag_send, ag_recv, cl_send, cl_recv, out_send, out_recv, copy_sem,
):
    seqs, span, wa = act.shape[1:]
    wc = cot.shape[3]
    rank = down.shape[1]
    c = lax.axis_index("client")
    r = lax.axis_index("row")

    barrier = pltpu.get_barrier_semaphore()

    def greet_row(k, _):
        pl.semaphore_signal(barrier, inc=1, device_id=(c, lax.rem(r + k, nr)), device_id_type=MESH)
        return 0

    def greet_client(k, _):
        pl.semaphore_signal(barrier, inc=1, device_id=(lax.rem(c + k, nc), r), device_id_type=MESH)
        return 0

    lax.fori_loop(1, nr, greet_row, 0)
    lax.fori_loop(1, nc, greet_client, 0)

    small = [
        pltpu.make_async_copy(up.at[0], adapt.at[:, pl.ds(0, wc)], small_sem.at[0]),
        pltpu.make_async_copy(down.at[0], adapt.at[:, pl.ds(wc, wa)], small_sem.at[1]),
        pltpu.make_async_copy(lens, lens_s, small_sem.at[2]),
    ]
    for copy in small:
        copy.start()
    loads = []
    for e in range(seqs):
        loads.append((
            pltpu.make_async_copy(cot.at[0, e], data.at[e, :, pl.ds(0, wc)], load_sem.at[2 * e]),
            pltpu.make_async_copy(act.at[0, e], data.at[e, :, pl.ds(wc, wa)], load_sem.at[2 * e + 1]),
        ))
        for copy in loads[e]:
            copy.start()
    for copy in small:
        copy.wait()

    half = span // 2
    rows = 2 * rank // 4

    def scatter(e, k):
        to = lax.rem(r + k, nr)
        return pltpu.make_async_remote_copy(
            src_ref=part.at[e, to], dst_ref=arrived.at[e, k - 1],
            send_sem=rs_send.at[e], recv_sem=rs_recv.at[e],
            device_id=(c, to), device_id_type=MESH,
        )

    def spread(e, k):
        to = lax.rem(r + k, nr)
        return pltpu.make_async_remote_copy(
            src_ref=mine.at[e], dst_ref=tokens.at[e, r],
            send_sem=ag_send.at[e], recv_sem=ag_recv.at[e],
            device_id=(c, to), device_id_type=MESH,
        )

    for e in range(seqs):
        with jax.named_scope("project"):
            for copy in loads[e]:
                copy.wait()
            pulled = lax.dot_general(adapt[:, :wc], data[e, :, :wc], NT, preferred_element_type=F32)
            projected = lax.dot_general(adapt[:, wc:], data[e, :, wc:], NT, preferred_element_type=F32)
            for b in range(nr):
                source = projected if b < nr // 2 else pulled
                top, left = (b // 2) % 2 * rows, b % 2 * half
                part[e, b] = source[top:top + rows, left:left + half].astype(PART)
        if e == 0:
            with jax.named_scope("barrier"):
                pl.semaphore_wait(barrier, nr - 1 + nc - 1)
        for k in range(1, nr):
            scatter(e, k).start()

    position = lax.broadcasted_iota(jnp.int32, (1, half), 1) + lax.rem(r, 2) * half
    for e in range(seqs):
        with jax.named_scope("rowsum"):
            pltpu.make_async_remote_copy(
                src_ref=part.at[e, pl.ds(0, nr - 1)], dst_ref=arrived.at[e],
                send_sem=rs_send.at[e], recv_sem=rs_recv.at[e], device_id=(c, r), device_id_type=MESH,
            ).wait()
            total = part[e, r].astype(F32)
            for k in range(nr - 1):
                total += arrived[e, k].astype(F32)
            length = jnp.full((1, half), lens_s[0, e], jnp.int32)
            weight = (position < length).astype(F32) / length.astype(F32)
            mine[e] = (total * weight).astype(BF16)
            tokens[e, r] = mine[e]
        for k in range(1, nr):
            spread(e, k).start()

    for e in range(seqs):
        with jax.named_scope("rowgather"):
            pltpu.make_async_remote_copy(
                src_ref=tokens.at[e, pl.ds(0, nr - 1)], dst_ref=tokens.at[e, pl.ds(0, nr - 1)],
                send_sem=ag_send.at[e], recv_sem=ag_recv.at[e], device_id=(c, r), device_id_type=MESH,
            ).wait()

    def fishers(block):
        columns = pl.ds(pl.multiple_of(block * LANES, LANES), LANES)
        first = (block < wc // LANES).astype(jnp.int32)
        base = (1 - first) * (nr // 2)
        total = jnp.zeros((rank, LANES), F32)
        for e in range(seqs):
            lines = [
                jnp.concatenate([tokens[e, base + 2 * i], tokens[e, base + 2 * i + 1]], axis=1)
                for i in range(nr // 4)
            ]
            grad = jnp.dot(jnp.concatenate(lines, axis=0), data[e, :, columns], preferred_element_type=F32)
            total += grad * grad
        return total * adapt[:, columns].astype(F32), total

    def give(block, slot):
        return pltpu.make_async_remote_copy(
            src_ref=terms.at[slot], dst_ref=received.at[slot],
            send_sem=cl_send, recv_sem=cl_recv,
            device_id=(block, r), device_id_type=MESH,
        )

    def column(k, _):
        block = lax.rem(c + k, nc)
        weighted, fisher = fishers(block)
        terms[k - 1, :rank] = weighted.astype(BF16)
        terms[k - 1, rank:] = fisher.astype(BF16)
        give(block, k - 1).start()
        return 0

    with jax.named_scope("grads"):
        lax.fori_loop(1, nc, column, 0)
        weighted, fisher = fishers(c)

    with jax.named_scope("clientsum"):
        give(c, pl.ds(0, nc - 1)).wait()
        for k in range(nc - 1):
            weighted += received[k, :rank].astype(F32)
            fisher += received[k, rank:].astype(F32)
        merged[...] = (weighted / (fisher + EPS)).astype(BF16)

    def publish(k, _):
        pltpu.make_async_remote_copy(
            src_ref=merged, dst_ref=gathered.at[c],
            send_sem=out_send, recv_sem=out_recv,
            device_id=(lax.rem(c + k, nc), r), device_id_type=MESH,
        ).start()
        return 0

    lax.fori_loop(1, nc, publish, 0)
    gathered[c] = merged[...]
    with jax.named_scope("clientgather"):
        pltpu.make_async_remote_copy(
            src_ref=gathered.at[pl.ds(0, nc - 1)], dst_ref=gathered.at[pl.ds(0, nc - 1)],
            send_sem=out_send, recv_sem=out_recv, device_id=(c, r), device_id_type=MESH,
        ).wait()
    with jax.named_scope("writeout"):
        for b in range(nc):
            out[:, b * LANES:(b + 1) * LANES] = gathered[b]


def local(nc, nr, activations, cotangent, lengths, adapter_down, adapter_up):
    _, seqs, span, wa = activations.shape
    wc = cotangent.shape[3]
    rank = adapter_down.shape[1]
    width = wa + wc
    rows, half = 2 * rank // 4, span // 2
    hbm = pl.BlockSpec(memory_space=pl.ANY)
    out = pl.pallas_call(
        functools.partial(kernel, nc, nr),
        out_shape=jax.ShapeDtypeStruct((rank, width), BF16),
        in_specs=[hbm] * 5,
        out_specs=pl.BlockSpec(memory_space=pltpu.VMEM),
        scratch_shapes=[
            pltpu.VMEM((seqs, span, width), BF16),
            pltpu.VMEM((rank, width), BF16),
            pltpu.SMEM((1, seqs), jnp.int32),
            pltpu.VMEM((seqs, nr, rows, half), PART),
            pltpu.VMEM((seqs, nr - 1, rows, half), PART),
            pltpu.VMEM((seqs, rows, half), BF16),
            pltpu.VMEM((seqs, nr, rows, half), BF16),
            pltpu.VMEM((nc - 1, 2 * rank, LANES), BF16),
            pltpu.VMEM((nc - 1, 2 * rank, LANES), BF16),
            pltpu.VMEM((rank, LANES), BF16),
            pltpu.VMEM((nc, rank, LANES), BF16),
            pltpu.SemaphoreType.DMA((2 * seqs,)),
            pltpu.SemaphoreType.DMA((3,)),
            pltpu.SemaphoreType.DMA((seqs,)),
            pltpu.SemaphoreType.DMA((seqs,)),
            pltpu.SemaphoreType.DMA((seqs,)),
            pltpu.SemaphoreType.DMA((seqs,)),
            pltpu.SemaphoreType.DMA,
            pltpu.SemaphoreType.DMA,
            pltpu.SemaphoreType.DMA,
            pltpu.SemaphoreType.DMA,
            pltpu.SemaphoreType.DMA,
        ],
        compiler_params=pltpu.CompilerParams(
            collective_id=0, has_side_effects=True, vmem_limit_bytes=48 * 1024 * 1024
        ),
    )(activations, cotangent, lengths, adapter_down, adapter_up)
    return out[:, wc:], out[:, :wc]


def solution(mesh):
    in_specs = (
        P("client", None, None, "row"),
        P("client", None, None, "row"),
        P("client", None),
        P("client", None, "row"),
        P("client", None, "row"),
    )
    out_specs = (P(None, "row"), P(None, "row"))
    body = functools.partial(local, mesh.shape["client"], mesh.shape["row"])
    return jax.shard_map(body, mesh=mesh, in_specs=in_specs, out_specs=out_specs, check_vma=False)
```

```python
import functools

import jax
import jax.numpy as jnp
from jax import lax
from jax.experimental import pallas as pl
from jax.experimental.pallas import tpu as pltpu
from jax.sharding import PartitionSpec as P

EPS = 1e-06
MESH = pl.DeviceIdType.MESH
LANES = 128
F32 = jnp.float32
BF16 = jnp.bfloat16
NT = (((1,), (1,)), ((), ()))
NX, NL, NY = 4, 2, 4
NH, NCORE = 4, 2
PLANE = NL * NY
UP_BLOCKS = 27
SPAN = 7
PROJECTED, PULLED = 0, 1
FINISH_AT = 2


def hops(offset):
    dx, dl, dy = offset
    return min(dx, NX - dx) + dl + min(dy, NY - dy)


def kernel(
    act, cot, lens, down, up, out,
    data, adapt, lens_s, part, sibling, pair, arrived, tokens, terms, dterms, received, own, merged, gathered,
    load_sem, small_sem, ex_send, ex_recv, bc_send, bc_recv, tk_send, tk_recv,
    up_send, up_recv, dn_send, dn_recv, out_send, out_recv,
):
    seqs, span, wa = act.shape[1:]
    wc = cot.shape[3]
    rank = down.shape[1]
    half = rank // 2
    c = lax.axis_index("client")
    r = lax.axis_index("row")
    x, lo, y = c // PLANE, (c // NY) % NL, c % NY
    hi, core = r // NCORE, r % NCORE

    def client(offset):
        dx, dl, dy = offset
        return lax.rem(x + dx, NX) * PLANE + lax.rem(lo + dl, NL) * NY + lax.rem(y + dy, NY)

    def chip(k):
        return lax.rem(hi + k, NH) * NCORE + core

    offsets = [(dx, dl, dy) for dx in range(NX) for dl in range(NL) for dy in range(NY)]
    offsets = sorted(offsets, key=lambda o: -hops(o))[:-1]
    peers = [(c, hi * NCORE + 1 - core)] + [(c, chip(k)) for k in (2, 1, 3)]
    peers += [(client(o), r) for o in offsets]
    other = peers[0]

    small = [
        pltpu.make_async_copy(down.at[0], adapt.at[:, pl.ds(wc, wa)], small_sem.at[0]),
        pltpu.make_async_copy(up.at[0], adapt.at[:, pl.ds(0, wc)], small_sem.at[1]),
        pltpu.make_async_copy(lens, lens_s, small_sem.at[2]),
    ]
    load_act = pltpu.make_async_copy(act.at[0], data.at[:, :, pl.ds(wc, wa)], load_sem.at[seqs])
    load_cot = [
        pltpu.make_async_copy(cot.at[0, e], data.at[e, :, pl.ds(0, wc)], load_sem.at[e])
        for e in range(seqs)
    ]
    for copy in [small[0], load_act, small[1]] + load_cot + [small[2]]:
        copy.start()

    barrier = pltpu.get_barrier_semaphore()
    for peer in peers:
        pl.semaphore_signal(barrier, inc=1, device_id=peer, device_id_type=MESH)

    def remote(src, dst, send, recv, to):
        return pltpu.make_async_remote_copy(
            src_ref=src, dst_ref=dst, send_sem=send, recv_sem=recv, device_id=to, device_id_type=MESH
        )

    def exchange(step):
        if step == 0:
            return remote(part.at[PROJECTED, 1 - core], sibling.at[PROJECTED], ex_send.at[0], ex_recv.at[0], other)
        e = step - 1
        return remote(part.at[PULLED, 1 - core, e], sibling.at[PULLED, e], ex_send.at[step], ex_recv.at[step], other)

    def broadcast(step):
        exchange(step).wait_recv()
        if step == 0:
            pair[PROJECTED] = (part[PROJECTED, core] + sibling[PROJECTED]).astype(BF16)
        else:
            e = step - 1
            pair[PULLED, e] = (part[PULLED, core, e] + sibling[PULLED, e]).astype(BF16)
        for k in (2, 1, 3):
            if step == 0:
                src, dst = pair.at[PROJECTED], arrived.at[PROJECTED, k - 1]
            else:
                src, dst = pair.at[PULLED, e], arrived.at[PULLED, k - 1, e]
            remote(src, dst, bc_send.at[step], bc_recv.at[step], (c, chip(k))).start()

    def broadcast_all(step):
        if step == 0:
            ref = arrived.at[PROJECTED]
        else:
            ref = arrived.at[PULLED, :, step - 1]
        return remote(ref, ref, bc_send.at[step], bc_recv.at[step], other)

    def token_swap(kind):
        ref = tokens.at[kind, core]
        return remote(ref, ref, tk_send.at[kind], tk_recv.at[kind], other)

    def finish(kind):
        for step in ((0,) if kind == PROJECTED else range(1, 1 + seqs)):
            broadcast_all(step).wait_recv()
        position = lax.broadcasted_iota(jnp.int32, (1, span), 1)
        for e in range(seqs):
            total = part[kind, core, e] + sibling[kind, e]
            for k in range(NH - 1):
                total += arrived[kind, k, e].astype(F32)
            length = jnp.full((1, span), lens_s[0, e], jnp.int32)
            weight = (position < length).astype(F32) / length.astype(F32)
            tokens[kind, core, e] = (total * weight).astype(BF16)
        token_swap(kind).start()

    load_act.wait()
    small[0].wait()
    for e in range(seqs):
        projected = lax.dot_general(adapt[:, wc:], data[e, :, wc:], NT, preferred_element_type=F32)
        part[PROJECTED, 0, e] = projected[:half]
        part[PROJECTED, 1, e] = projected[half:]
    pl.semaphore_wait(barrier, len(peers))
    exchange(0).start()
    small[1].wait()
    for e in range(seqs):
        load_cot[e].wait()
        pulled = lax.dot_general(adapt[:, :wc], data[e, :, :wc], NT, preferred_element_type=F32)
        part[PULLED, 0, e] = pulled[:half]
        part[PULLED, 1, e] = pulled[half:]
        exchange(1 + e).start()
        broadcast(e)
    broadcast(seqs)
    small[2].wait()
    finish(PROJECTED)

    def fishers(kind, columns, width):
        total = jnp.zeros((rank, width), F32)
        for e in range(seqs):
            left = jnp.concatenate([tokens[kind, 0, e], tokens[kind, 1, e]], axis=0)
            grad = jnp.dot(left, data[e, :, columns], preferred_element_type=F32)
            total += grad * grad
        return (total * adapt[:, columns].astype(F32)).astype(BF16), total.astype(BF16)

    def units(weighted, fisher, b):
        columns = slice(b * LANES, (b + 1) * LANES)
        return [
            jnp.concatenate([weighted[h * half:(h + 1) * half, columns], fisher[h * half:(h + 1) * half, columns]], axis=0)
            for h in range(2)
        ]

    def is_whole(p, j):
        return j < jnp.where(p < NX - 1, 6, 4)

    def up_index(p, j):
        return jnp.where(p < NX - 1, jnp.minimum(j, SPAN - 1), jnp.where(j < 4, j + 1, 5 + (j - 4) // 2))

    def give_up(stage, offset):
        to = client(offset)
        p, j = to // PLANE, to % PLANE
        index = up_index(p, j)
        slot = offset[0] * PLANE + offset[1] * NY + offset[2] - 1

        @pl.when(is_whole(p, j))
        def _():
            remote(terms.at[stage, index], received.at[pl.ds(2 * slot, 2)], up_send, up_recv, (to, r)).start()

        @pl.when(jnp.logical_not(is_whole(p, j)))
        def _():
            remote(terms.at[stage, index, j % 2], received.at[2 * slot], up_send, up_recv, (to, r)).start()

    token_swap(PROJECTED).wait_recv()
    steps = (2, 1, 3, 0)

    def up_stage(stage):
        dx = steps[stage]
        p = lax.rem(x + dx, NX)
        first = jnp.minimum(p * SPAN, UP_BLOCKS - SPAN)
        columns = pl.ds(pl.multiple_of(first * LANES, LANES), SPAN * LANES)
        weighted, fisher = fishers(PROJECTED, columns, SPAN * LANES)
        for b in range(SPAN):
            for h, unit in enumerate(units(weighted, fisher, b)):
                terms[stage, b, h] = unit
        for offset in offsets:
            if offset[0] == dx:
                give_up(stage, offset)

    for stage in range(NX):
        if stage == FINISH_AT:
            finish(PULLED)
        up_stage(stage)

    token_swap(PULLED).wait_recv()
    weighted, fisher = fishers(PULLED, pl.ds(wc, wa), wa)
    for b in range(wa // LANES):
        for h, unit in enumerate(units(weighted, fisher, b)):
            dterms[2 * b + h] = unit
    down_units = 2 * (wa // LANES)
    for k in range(down_units):
        n = lax.rem(c + k, down_units)
        to = jnp.minimum(n // 2, NX - 1) * PLANE + jnp.where(n < 6, 6 + n % 2, n - 2)
        dx, dl, dy = lax.rem(to // PLANE - x + NX, NX), lax.rem(to // NY % NL - lo + NL, NL), lax.rem(to % NY - y + NY, NY)
        slot = dx * PLANE + dl * NY + dy - 1

        @pl.when(c != to)
        def _():
            remote(dterms.at[n], received.at[2 * slot + 1], dn_send, dn_recv, (to, r)).start()

    j = c % PLANE
    whole = is_whole(x, j)
    split = jnp.logical_not(whole)
    peers_n = NX * PLANE - 1
    mine = terms.at[NX - 1, up_index(x, j)]

    @pl.when(whole)
    def _():
        remote(received, received, up_send, up_recv, other).wait_recv()
        own[...] = mine[...]

    @pl.when(split)
    def _():
        ref = received.at[pl.ds(0, peers_n)]
        remote(ref, ref, up_send, up_recv, other).wait_recv()
        remote(ref, ref, dn_send, dn_recv, other).wait_recv()
        own[0] = mine[j % 2]
        own[1] = dterms[jnp.where(x < NX - 1, 2 * x + j % 2, j + 2)]

    for u in range(2):
        total = own[u].astype(F32)
        for slot in range(peers_n):
            total += received[2 * slot + u].astype(F32)
        merged[u] = (total[:half] / (total[half:] + EPS)).astype(BF16)
    for offset in offsets:
        remote(merged, gathered.at[c], out_send, out_recv, (client(offset), r)).start()
    gathered[c] = merged[...]

    for step in range(1 + seqs):
        exchange(step).wait_send()
        broadcast_all(step).wait_send()
    for kind in (PROJECTED, PULLED):
        token_swap(kind).wait_send()

    def sent(n, sem):
        ref = received.at[pl.ds(0, n)]
        remote(ref, ref, sem, sem, other).wait_send()

    @pl.when(whole)
    def _():
        sent(2 * 21 + 10, up_send)
        sent(10, dn_send)

    @pl.when(split)
    def _():
        sent(2 * 22 + 9, up_send)
        sent(9, dn_send)

    ref = gathered.at[pl.ds(0, peers_n)]
    remote(ref, ref, out_send, out_recv, other).wait()
    for owner in range(NX * PLANE):
        p, j = owner // PLANE, owner % PLANE
        if j < (6 if p < NX - 1 else 4):
            block = SPAN * p + j
            for h in range(2):
                out[h * half:(h + 1) * half, block * LANES:(block + 1) * LANES] = gathered[owner, h]
        else:
            block, dblock = (SPAN * p + 6, p) if p < NX - 1 else (25 + (j - 4) // 2, 3 + (j - 4) // 2)
            h = j % 2
            out[h * half:(h + 1) * half, block * LANES:(block + 1) * LANES] = gathered[owner, 0]
            out[h * half:(h + 1) * half, wc + dblock * LANES:wc + (dblock + 1) * LANES] = gathered[owner, 1]


def local(activations, cotangent, lengths, adapter_down, adapter_up):
    _, seqs, span, wa = activations.shape
    wc = cotangent.shape[3]
    rank = adapter_down.shape[1]
    half = rank // 2
    width = wa + wc
    owners = NX * PLANE
    hbm = pl.BlockSpec(memory_space=pl.ANY)
    dma = pltpu.SemaphoreType.DMA
    out = pl.pallas_call(
        kernel,
        out_shape=jax.ShapeDtypeStruct((rank, width), BF16),
        in_specs=[hbm] * 5,
        out_specs=pl.BlockSpec(memory_space=pltpu.VMEM),
        scratch_shapes=[
            pltpu.VMEM((seqs, span, width), BF16),
            pltpu.VMEM((rank, width), BF16),
            pltpu.SMEM((1, seqs), jnp.int32),
            pltpu.VMEM((2, 2, seqs, half, span), F32),
            pltpu.VMEM((2, seqs, half, span), F32),
            pltpu.VMEM((2, seqs, half, span), BF16),
            pltpu.VMEM((2, NH - 1, seqs, half, span), BF16),
            pltpu.VMEM((2, 2, seqs, half, span), BF16),
            pltpu.VMEM((NX, SPAN, 2, rank, LANES), BF16),
            pltpu.VMEM((2 * (wa // LANES), rank, LANES), BF16),
            pltpu.VMEM((2 * (owners - 1), rank, LANES), BF16),
            pltpu.VMEM((2, rank, LANES), BF16),
            pltpu.VMEM((2, half, LANES), BF16),
            pltpu.VMEM((owners, 2, half, LANES), BF16),
            dma((seqs + 1,)), dma((3,)),
            dma((seqs + 1,)), dma((seqs + 1,)), dma((seqs + 1,)), dma((seqs + 1,)), dma((2,)), dma((2,)),
            dma, dma, dma, dma, dma, dma,
        ],
        compiler_params=pltpu.CompilerParams(
            collective_id=0, has_side_effects=True, vmem_limit_bytes=48 * 1024 * 1024
        ),
    )(*(pltpu.with_memory_space_constraint(a, pltpu.HBM) for a in (activations, cotangent, lengths, adapter_down, adapter_up)))
    return out[:, wc:], out[:, :wc]


def solution(mesh):
    in_specs = (
        P("client", None, None, "row"),
        P("client", None, None, "row"),
        P("client", None),
        P("client", None, "row"),
        P("client", None, "row"),
    )
    out_specs = (P(None, "row"), P(None, "row"))
    return jax.shard_map(local, mesh=mesh, in_specs=in_specs, out_specs=out_specs, check_vma=False)
```

```python
import jax
import jax.numpy as jnp
from jax import lax
from jax.experimental import pallas as pl
from jax.experimental.pallas import tpu as pltpu
from jax.sharding import PartitionSpec as P

EPS = 1e-06
MESH = pl.DeviceIdType.MESH
LANES = 128
F32 = jnp.float32
BF16 = jnp.bfloat16
NT = (((1,), (1,)), ((), ()))
NX, NL, NY = 4, 2, 4
NH, NCORE = 4, 2
PLANE = NL * NY
OWNERS = NX * PLANE
UP_BLOCKS = 27
SPAN = 7
PROJECTED, PULLED = 0, 1
FINISH_AT = 3


def pick(v, a, b, c, d):
    return jnp.where(v == 0, a, jnp.where(v == 1, b, jnp.where(v == 2, c, d)))


def kernel(
    act, cot, lens, down, up, out,
    data, adapt, lens_s, part, sibling, pair, arrived, tokens, terms, dterms, factors, fishers_in, own, merged, gathered,
    load_sem, small_sem, ex_send, ex_recv, bc_send, bc_recv, tk_send, tk_recv,
    a_send, a_recv, f_send, f_recv, out_send, out_recv, plane_sem, all_sem,
):
    seqs, span, wa = act.shape[1:]
    wc = cot.shape[3]
    rank = down.shape[1]
    half = rank // 2
    mid = seqs // 2
    c = lax.axis_index("client")
    r = lax.axis_index("row")
    x, lo, y = c // PLANE, (c // NY) % NL, c % NY
    hi, core = r // NCORE, r % NCORE

    def client(dx, dl, dy):
        return lax.rem(x + dx, NX) * PLANE + lax.rem(lo + dl, NL) * NY + lax.rem(y + dy, NY)

    def chip(k):
        return (c, lax.rem(hi + k, NH) * NCORE + core)

    def target(k):
        v, q = k // PLANE, k % PLANE
        return client(pick(v, 2, 1, 3, 0), 1 - q // NY, pick(q % NY, 2, 1, 3, 0))

    def slot_at(to):
        dx, dl, dy = lax.rem(to // PLANE - x + NX, NX), lax.rem(to // NY % NL - lo + NL, NL), lax.rem(to % NY - y + NY, NY)
        return pick(dx, 3, 1, 0, 2) * PLANE + (1 - dl) * NY + pick(dy, 3, 1, 0, 2)

    def rows(unit, n):
        return pl.ds(pl.multiple_of(unit * half, half), n * half)

    def lanes(block):
        return pl.ds(pl.multiple_of(block * LANES, LANES), LANES)

    def is_whole(p, j):
        return j < jnp.where(p < NX - 1, 6, 4)

    def up_block(p, j):
        return jnp.where(p < NX - 1, p * SPAN + jnp.minimum(j, SPAN - 1), jnp.where(j < 4, 21 + j, 25 + (j - 4) // 2))

    def down_block(p, j):
        return jnp.where(p < NX - 1, p, 3 + (j - 4) // 2)

    def first_block(p):
        return jnp.minimum(p * SPAN, UP_BLOCKS - SPAN)

    other = (c, hi * NCORE + 1 - core)
    peers = [other] + [chip(k) for k in (2, 1, 3)]
    along_y = [(client(0, 0, k), r) for k in (2, 1, 3)]
    peers += [(client(k, 0, 0), r) for k in (2, 1, 3)] + along_y + [(client(0, 1, 0), r)]

    small = [
        pltpu.make_async_copy(down.at[0], adapt.at[:, pl.ds(wc, wa)], small_sem.at[0]),
        pltpu.make_async_copy(up.at[0], adapt.at[:, pl.ds(0, wc)], small_sem.at[1]),
        pltpu.make_async_copy(lens, lens_s, small_sem.at[2]),
    ]
    load_act = pltpu.make_async_copy(act.at[0], data.at[:, :, pl.ds(wc, wa)], load_sem.at[seqs])

    def load_cot(e):
        return pltpu.make_async_copy(cot.at[0, e], data.at[e, :, pl.ds(0, wc)], load_sem.at[e])

    for copy in [small[0], load_act, small[1]] + [load_cot(e) for e in range(seqs)] + [small[2]]:
        copy.start()

    barrier = pltpu.get_barrier_semaphore()
    for peer in peers:
        pl.semaphore_signal(barrier, inc=1, device_id=peer, device_id_type=MESH)

    def remote(src, dst, send, recv, to):
        return pltpu.make_async_remote_copy(
            src_ref=src, dst_ref=dst, send_sem=send, recv_sem=recv, device_id=to, device_id_type=MESH
        )

    def piece(step):
        return (PROJECTED, pl.ds(0, seqs)) if step == 0 else (PULLED, pl.ds((step - 1) * mid, mid))

    def exchange(step):
        kind, which = piece(step)
        return remote(part.at[kind, 1 - core, which], sibling.at[kind, which], ex_send.at[step], ex_recv.at[step], other)

    def broadcast(step):
        kind, which = piece(step)
        exchange(step).wait_recv()
        pair[kind, which] = (part[kind, core, which] + sibling[kind, which]).astype(BF16)
        for k in (2, 1, 3):
            remote(pair.at[kind, which], arrived.at[kind, k - 1, which], bc_send.at[step], bc_recv.at[step], chip(k)).start()

    def broadcast_all(step):
        kind, which = piece(step)
        ref = arrived.at[kind, :, which]
        return remote(ref, ref, bc_send.at[step], bc_recv.at[step], other)

    def token_swap(kind):
        ref = tokens.at[kind, core]
        return remote(ref, ref, tk_send.at[kind], tk_recv.at[kind], other)

    def finish(kind):
        for step in ((0,) if kind == PROJECTED else (1, 2)):
            broadcast_all(step).wait_recv()
        position = lax.broadcasted_iota(jnp.int32, (1, span), 1)
        for e in range(seqs):
            total = part[kind, core, e] + sibling[kind, e]
            for k in range(NH - 1):
                total += arrived[kind, k, e].astype(F32)
            length = jnp.full((1, span), lens_s[0, e], jnp.int32)
            weight = (position < length).astype(F32) / length.astype(F32)
            tokens[kind, core, e] = (total * weight).astype(BF16)
        token_swap(kind).start()

    load_act.wait()
    small[0].wait()
    for e in range(seqs):
        projected = lax.dot_general(adapt[:, wc:], data[e, :, wc:], NT, preferred_element_type=F32)
        part[PROJECTED, 0, e] = projected[:half]
        part[PROJECTED, 1, e] = projected[half:]
    small[1].wait()

    def pull(e, _):
        load_cot(e).wait()
        pulled = lax.dot_general(adapt[:, :wc], data[e, :, :wc], NT, preferred_element_type=F32)
        part[PULLED, 0, e] = pulled[:half]
        part[PULLED, 1, e] = pulled[half:]

        @pl.when(e == mid - 1)
        def _():
            pl.semaphore_wait(barrier, len(peers))
            exchange(0).start()
            exchange(1).start()
            for peer in along_y:
                pl.semaphore_signal(plane_sem, inc=1, device_id=peer, device_id_type=MESH)

        @pl.when(e == mid)
        def _():
            broadcast(0)
            broadcast(1)

        return 0

    lax.fori_loop(0, seqs, pull, 0)
    exchange(2).start()
    pl.semaphore_wait(plane_sem, NY - 1)
    pl.semaphore_signal(all_sem, inc=1, device_id=(client(0, 1, 0), r), device_id_type=MESH)
    broadcast(2)
    small[2].wait()
    pl.semaphore_wait(all_sem, 1)

    def give_factors(k, _):
        to = target(k)
        p, j = to // PLANE, to % PLANE
        block, h = up_block(p, j), j % 2

        @pl.when(is_whole(p, j))
        def _():
            remote(adapt.at[:, lanes(block)], factors.at[rows(2 * k, 2)], a_send, a_recv, (to, r)).start()

        @pl.when(jnp.logical_not(is_whole(p, j)))
        def _():
            remote(adapt.at[rows(h, 1), lanes(block)], factors.at[rows(2 * k, 1)], a_send, a_recv, (to, r)).start()
            block2 = wc // LANES + down_block(p, j)
            remote(adapt.at[rows(h, 1), lanes(block2)], factors.at[rows(2 * k + 1, 1)], a_send, a_recv, (to, r)).start()

        return 0

    lax.fori_loop(0, OWNERS - 1, give_factors, 0)
    finish(PROJECTED)

    def fishers(kind, columns, width):
        total = jnp.zeros((rank, width), F32)
        for e in range(seqs):
            left = jnp.concatenate([tokens[kind, 0, e], tokens[kind, 1, e]], axis=0)
            grad = jnp.dot(left, data[e, :, columns], preferred_element_type=F32)
            total += grad * grad
        return total.astype(BF16)

    token_swap(PROJECTED).wait_recv()

    def up_stage(stage, _):
        @pl.when(stage == FINISH_AT)
        def _():
            finish(PULLED)

        p = lax.rem(x + pick(stage, 2, 1, 3, 0), NX)
        first = first_block(p)
        fisher = fishers(PROJECTED, pl.ds(pl.multiple_of(first * LANES, LANES), SPAN * LANES), SPAN * LANES)
        for b in range(SPAN):
            terms[stage, b * rank:(b + 1) * rank] = fisher[:, b * LANES:(b + 1) * LANES]

        def give(q, _):
            k = stage * PLANE + q
            to = target(k)
            j = to % PLANE
            unit = 2 * (up_block(p, j) - first)

            @pl.when(is_whole(p, j))
            def _():
                remote(terms.at[stage, rows(unit, 2)], fishers_in.at[rows(2 * k, 2)], f_send, f_recv, (to, r)).start()

            @pl.when(jnp.logical_not(is_whole(p, j)))
            def _():
                remote(terms.at[stage, rows(unit + j % 2, 1)], fishers_in.at[rows(2 * k, 1)], f_send, f_recv, (to, r)).start()

            return 0

        lax.fori_loop(0, jnp.where(stage == NX - 1, PLANE - 1, PLANE), give, 0)
        return 0

    lax.fori_loop(0, NX, up_stage, 0)

    token_swap(PULLED).wait_recv()
    fisher = fishers(PULLED, pl.ds(wc, wa), wa)
    for b in range(wa // LANES):
        dterms[b * rank:(b + 1) * rank] = fisher[:, b * LANES:(b + 1) * LANES]
    units = 2 * (wa // LANES)

    def give_down(k, _):
        n = lax.rem(c + k, units)
        to = jnp.minimum(n // 2, NX - 1) * PLANE + jnp.where(n < 6, 6 + n % 2, n - 2)

        @pl.when(c != to)
        def _():
            remote(dterms.at[rows(n, 1)], fishers_in.at[rows(2 * slot_at(to) + 1, 1)], f_send, f_recv, (to, r)).start()

        return 0

    lax.fori_loop(0, units, give_down, 0)

    j = c % PLANE
    whole = is_whole(x, j)
    unit = 2 * (up_block(x, j) - first_block(x))

    @pl.when(whole)
    def _():
        own[0] = terms[NX - 1, rows(unit, 2)]
        own[1] = adapt[:, lanes(up_block(x, j))]

    @pl.when(jnp.logical_not(whole))
    def _():
        block = down_block(x, j)
        own[0, :half] = terms[NX - 1, rows(unit + j % 2, 1)]
        own[0, half:] = dterms[rows(2 * block + j % 2, 1)]
        own[1, :half] = adapt[rows(j % 2, 1), lanes(up_block(x, j))]
        own[1, half:] = adapt[rows(j % 2, 1), lanes(wc // LANES + block)]

    remote(factors, factors, a_send, a_recv, other).wait_recv()
    remote(fishers_in, fishers_in, f_send, f_recv, other).wait_recv()
    total = own[0].astype(F32)
    weighted = total * own[1].astype(F32)

    def add(k, sums):
        fisher = fishers_in[rows(2 * k, 2)].astype(F32)
        return sums[0] + fisher, sums[1] + fisher * factors[rows(2 * k, 2)].astype(F32)

    total, weighted = lax.fori_loop(0, OWNERS - 1, add, (total, weighted), unroll=True)
    merged[...] = (weighted / (total + EPS)).astype(BF16)

    def publish(k, _):
        remote(merged, gathered.at[rows(2 * c, 2)], out_send, out_recv, (target(k), r)).start()
        return 0

    lax.fori_loop(0, OWNERS - 1, publish, 0)
    gathered[rows(2 * c, 2)] = merged[...]

    for step in range(3):
        exchange(step).wait_send()
        broadcast_all(step).wait_send()
    for kind in (PROJECTED, PULLED):
        token_swap(kind).wait_send()
    remote(factors, factors, a_send, a_recv, other).wait_send()
    remote(fishers_in, fishers_in, f_send, f_recv, other).wait_send()
    ref = gathered.at[pl.ds(0, rank * (OWNERS - 1))]
    remote(ref, ref, out_send, out_recv, other).wait()
    for owner in range(OWNERS):
        p, j = owner // PLANE, owner % PLANE
        h = j % 2
        if j < (6 if p < NX - 1 else 4):
            block = SPAN * p + j
            out[:, block * LANES:(block + 1) * LANES] = gathered[owner * rank:(owner + 1) * rank]
        else:
            block, dblock = (SPAN * p + 6, p) if p < NX - 1 else (25 + (j - 4) // 2, 3 + (j - 4) // 2)
            dblock += wc // LANES
            out[h * half:(h + 1) * half, block * LANES:(block + 1) * LANES] = gathered[owner * rank:owner * rank + half]
            out[h * half:(h + 1) * half, dblock * LANES:(dblock + 1) * LANES] = gathered[owner * rank + half:(owner + 1) * rank]


def local(*args):
    activations, cotangent, lengths, adapter_down, adapter_up = args
    _, seqs, span, wa = activations.shape
    wc = cotangent.shape[3]
    rank = adapter_down.shape[1]
    half = rank // 2
    width = wa + wc
    dma = pltpu.SemaphoreType.DMA
    out = pl.pallas_call(
        kernel,
        out_shape=jax.ShapeDtypeStruct((rank, width), BF16),
        in_specs=[pl.BlockSpec(memory_space=pl.ANY)] * 5,
        out_specs=pl.BlockSpec(memory_space=pltpu.VMEM),
        scratch_shapes=[
            pltpu.VMEM((seqs, span, width), BF16),
            pltpu.VMEM((rank, width), BF16),
            pltpu.SMEM((1, seqs), jnp.int32),
            pltpu.VMEM((2, 2, seqs, half, span), F32),
            pltpu.VMEM((2, seqs, half, span), F32),
            pltpu.VMEM((2, seqs, half, span), BF16),
            pltpu.VMEM((2, NH - 1, seqs, half, span), BF16),
            pltpu.VMEM((2, 2, seqs, half, span), BF16),
            pltpu.VMEM((NX, SPAN * rank, LANES), BF16),
            pltpu.VMEM((wa // LANES * rank, LANES), BF16),
            pltpu.VMEM((rank * (OWNERS - 1), LANES), BF16),
            pltpu.VMEM((rank * (OWNERS - 1), LANES), BF16),
            pltpu.VMEM((2, rank, LANES), BF16),
            pltpu.VMEM((rank, LANES), BF16),
            pltpu.VMEM((rank * OWNERS, LANES), BF16),
            dma((seqs + 1,)), dma((3,)), dma((3,)), dma((3,)), dma((3,)), dma((3,)), dma((2,)), dma((2,)),
            dma, dma, dma, dma, dma, dma, pltpu.SemaphoreType.REGULAR, pltpu.SemaphoreType.REGULAR,
        ],
        compiler_params=pltpu.CompilerParams(
            collective_id=0, has_side_effects=True, vmem_limit_bytes=48 * 1024 * 1024
        ),
    )(*(pltpu.with_memory_space_constraint(a, pltpu.HBM) for a in args))
    return out[:, wc:], out[:, :wc]


def solution(mesh):
    in_specs = (
        P("client", None, None, "row"),
        P("client", None, None, "row"),
        P("client", None),
        P("client", None, "row"),
        P("client", None, "row"),
    )
    out_specs = (P(None, "row"), P(None, "row"))
    return jax.shard_map(local, mesh=mesh, in_specs=in_specs, out_specs=out_specs, check_vma=False)
```

```python
import functools

import functools

import jax
import jax.numpy as jnp
from jax import lax
from jax.experimental import pallas as pl
from jax.experimental.pallas import tpu as pltpu
from jax.sharding import PartitionSpec as P

EPS = 1e-06
MESH = pl.DeviceIdType.MESH
LANES = 128
F32 = jnp.float32
BF16 = jnp.bfloat16
NT = (((1,), (1,)), ((), ()))
NX, NL, NY = 4, 2, 4
NH, NCORE = 4, 2
PLANE = NL * NY
OWNERS = NX * PLANE
UP_BLOCKS = 27
SPAN = 7
PROJECTED, PULLED = 0, 1
FINISH_AT = 2
SPLITS = (2, 2)
FIRST = 3


def pick(v, a, b, c, d):
    return jnp.where(v == 0, a, jnp.where(v == 1, b, jnp.where(v == 2, c, d)))


def kernel(
    act, cot, lens, down, up, out,
    data, adapt, lens_s, part, sibling, pair, arrived, tokens, terms, dterms, factors, fishers_in, own, merged, gathered,
    load_sem, small_sem, ex_send, ex_recv, bc_send, bc_recv, tk_send, tk_recv,
    a_send, a_recv, f_send, f_recv, out_send, out_recv, plane_sem, all_sem,
):
    seqs, span, wa = act.shape[1:]
    wc = cot.shape[3]
    rank = down.shape[1]
    half = rank // 2
    c = lax.axis_index("client")
    r = lax.axis_index("row")
    x, lo, y = c // PLANE, (c // NY) % NL, c % NY
    hi, core = r // NCORE, r % NCORE

    def client(dx, dl, dy):
        return lax.rem(x + dx, NX) * PLANE + lax.rem(lo + dl, NL) * NY + lax.rem(y + dy, NY)

    def chip(k):
        return (c, lax.rem(hi + k, NH) * NCORE + core)

    xs = [lax.rem(x + d, NX) * PLANE for d in (2, 1, 3, 0)]
    ls = [lax.rem(lo + d, NL) * NY for d in (1, 0)]
    ys = [lax.rem(y + d, NY) for d in (2, 1, 3, 0)]

    def target(k):
        if isinstance(k, int):
            return xs[k // PLANE] + ls[k % PLANE // NY] + ys[k % NY]
        v, q = k // PLANE, k % PLANE
        return client(pick(v, 2, 1, 3, 0), 1 - q // NY, pick(q % NY, 2, 1, 3, 0))

    def slot_at(to):
        dx, dl, dy = lax.rem(to // PLANE - x + NX, NX), lax.rem(to // NY % NL - lo + NL, NL), lax.rem(to % NY - y + NY, NY)
        return pick(dx, 3, 1, 0, 2) * PLANE + (1 - dl) * NY + pick(dy, 3, 1, 0, 2)

    def rows(unit, n):
        return pl.ds(pl.multiple_of(unit * half, half), n * half)

    def lanes(block):
        return pl.ds(pl.multiple_of(block * LANES, LANES), LANES)

    def is_whole(p, j):
        return j < jnp.where(p < NX - 1, 6, 4)

    def up_block(p, j):
        return jnp.where(p < NX - 1, p * SPAN + jnp.minimum(j, SPAN - 1), jnp.where(j < 4, 21 + j, 25 + (j - 4) // 2))

    def down_block(p, j):
        return jnp.where(p < NX - 1, p, 3 + (j - 4) // 2)

    def first_block(p):
        return jnp.minimum(p * SPAN, UP_BLOCKS - SPAN)

    other = (c, hi * NCORE + 1 - core)
    peers = [other] + [chip(k) for k in (2, 1, 3)]
    along_y = [(client(0, 0, k), r) for k in (2, 1, 3)]
    peers += [(client(k, 0, 0), r) for k in (2, 1, 3)] + along_y + [(client(0, 1, 0), r)]

    small = [
        pltpu.make_async_copy(down.at[0], adapt.at[:, pl.ds(wc, wa)], small_sem.at[0]),
        pltpu.make_async_copy(up.at[0], adapt.at[:, pl.ds(0, wc)], small_sem.at[1]),
        pltpu.make_async_copy(lens, lens_s, small_sem.at[2]),
    ]
    load_act = pltpu.make_async_copy(act.at[0], data.at[:, :, pl.ds(wc, wa)], load_sem.at[seqs])

    def load_cot(e):
        return pltpu.make_async_copy(cot.at[0, e], data.at[e, :, pl.ds(0, wc)], load_sem.at[e])

    loads = [small[0], load_act, small[1]] + [load_cot(e) for e in range(seqs)] + [small[2]]
    for copy in loads[:FIRST]:
        copy.start()

    barrier = pltpu.get_barrier_semaphore()
    for peer in peers:
        pl.semaphore_signal(barrier, inc=1, device_id=peer, device_id_type=MESH)
    for copy in loads[FIRST:]:
        copy.start()

    def remote(src, dst, send, recv, to):
        return pltpu.make_async_remote_copy(
            src_ref=src, dst_ref=dst, send_sem=send, recv_sem=recv, device_id=to, device_id_type=MESH
        )

    ends = [sum(SPLITS[:i + 1]) for i in range(len(SPLITS))]
    steps = 1 + len(SPLITS)

    def piece(step):
        return (PROJECTED, pl.ds(0, seqs)) if step == 0 else (PULLED, pl.ds(ends[step - 1] - SPLITS[step - 1], SPLITS[step - 1]))

    def exchange(step):
        kind, which = piece(step)
        return remote(part.at[kind, 1 - core, which], sibling.at[kind, which], ex_send.at[step], ex_recv.at[step], other)

    def broadcast(step):
        kind, which = piece(step)
        exchange(step).wait_recv()
        pair[kind, which] = (part[kind, core, which] + sibling[kind, which]).astype(BF16)
        for k in (2, 1, 3):
            remote(pair.at[kind, which], arrived.at[kind, k - 1, which], bc_send.at[step], bc_recv.at[step], chip(k)).start()

    def broadcast_all(step):
        kind, which = piece(step)
        ref = arrived.at[kind, :, which]
        return remote(ref, ref, bc_send.at[step], bc_recv.at[step], other)

    def token_swap(kind):
        ref = tokens.at[kind, core]
        return remote(ref, ref, tk_send.at[kind], tk_recv.at[kind], other)

    def finish(kind):
        for step in ((0,) if kind == PROJECTED else range(1, steps)):
            broadcast_all(step).wait_recv()
        position = lax.broadcasted_iota(jnp.int32, (1, span), 1)
        for e in range(seqs):
            total = part[kind, core, e] + sibling[kind, e]
            for k in range(NH - 1):
                total += arrived[kind, k, e].astype(F32)
            length = jnp.full((1, span), lens_s[0, e], jnp.int32)
            weight = (position < length).astype(F32) / length.astype(F32)
            tokens[kind, core, e] = (total * weight).astype(BF16)
        token_swap(kind).start()

    def meet():
        pl.semaphore_wait(barrier, len(peers))
        exchange(0).start()
        for peer in along_y:
            pl.semaphore_signal(plane_sem, inc=1, device_id=peer, device_id_type=MESH)

    load_act.wait()
    small[0].wait()
    for e in range(seqs):
        projected = lax.dot_general(adapt[:, wc:], data[e, :, wc:], NT, preferred_element_type=F32)
        part[PROJECTED, 0, e] = projected[:half]
        part[PROJECTED, 1, e] = projected[half:]
    small[1].wait()

    def pull(e, _):
        load_cot(e).wait()
        pulled = lax.dot_general(adapt[:, :wc], data[e, :, :wc], NT, preferred_element_type=F32)
        part[PULLED, 0, e] = pulled[:half]
        part[PULLED, 1, e] = pulled[half:]

        pl.when(e == 0)(meet)

        for step in range(1, steps):
            pl.when(e == sent_at[step])(exchange(step).start)
        for step in range(steps):
            if cast_at[step] < seqs:
                pl.when(e == cast_at[step])(functools.partial(broadcast, step))
        return 0

    sent_at = [0] + [end - 1 for end in ends]
    cast_at = [0] + [end for end in ends]
    lax.fori_loop(0, seqs, pull, 0)
    for step in range(steps):
        if cast_at[step] >= seqs:
            broadcast(step)
    pl.semaphore_wait(plane_sem, NY - 1)
    pl.semaphore_signal(all_sem, inc=1, device_id=(client(0, 1, 0), r), device_id_type=MESH)
    small[2].wait()

    def give_factors(v, _):
        p = lax.rem(x + pick(v, 2, 1, 3, 0), NX)
        for q in range(PLANE):
            if q < PLANE - 1:
                give_factor(v, p, q)
            else:
                pl.when(v < NX - 1)(functools.partial(give_factor, v, p, q))
        return 0

    def give_factor(v, p, q):
        k = v * PLANE + q
        j = ls[q // NY] + ys[q % NY]
        to = p * PLANE + j
        block, h = up_block(p, j), j % 2

        @pl.when(is_whole(p, j))
        def _():
            remote(adapt.at[:, lanes(block)], factors.at[rows(2 * k, 2)], a_send, a_recv, (to, r)).start()

        @pl.when(jnp.logical_not(is_whole(p, j)))
        def _():
            remote(adapt.at[rows(h, 1), lanes(block)], factors.at[rows(2 * k, 1)], a_send, a_recv, (to, r)).start()
            block2 = wc // LANES + down_block(p, j)
            remote(adapt.at[rows(h, 1), lanes(block2)], factors.at[rows(2 * k + 1, 1)], a_send, a_recv, (to, r)).start()


    pl.semaphore_wait(all_sem, 1)
    lax.fori_loop(0, NX, give_factors, 0)
    finish(PROJECTED)

    def fishers(kind, columns, width):
        total = jnp.zeros((rank, width), F32)
        for e in range(seqs):
            left = jnp.concatenate([tokens[kind, 0, e], tokens[kind, 1, e]], axis=0)
            grad = jnp.dot(left, data[e, :, columns], preferred_element_type=F32)
            total += grad * grad
        return total.astype(BF16)

    token_swap(PROJECTED).wait_recv()

    units = 2 * (wa // LANES)

    def down_stage():
        token_swap(PULLED).wait_recv()
        fisher = fishers(PULLED, pl.ds(wc, wa), wa)
        for b in range(wa // LANES):
            dterms[b * rank:(b + 1) * rank] = fisher[:, b * LANES:(b + 1) * LANES]

        def give_down(k, _):
            n = lax.rem(c + k, units)
            to = jnp.minimum(n // 2, NX - 1) * PLANE + jnp.where(n < 6, 6 + n % 2, n - 2)

            @pl.when(c != to)
            def _():
                remote(dterms.at[rows(n, 1)], fishers_in.at[rows(2 * slot_at(to) + 1, 1)], f_send, f_recv, (to, r)).start()

            return 0

        lax.fori_loop(0, units, give_down, 0)

    def up_stage(stage, _):
        @pl.when(stage == FINISH_AT)
        def _():
            finish(PULLED)

        p = lax.rem(x + pick(stage, 2, 1, 3, 0), NX)
        first = first_block(p)
        fisher = fishers(PROJECTED, pl.ds(pl.multiple_of(first * LANES, LANES), SPAN * LANES), SPAN * LANES)
        for b in range(SPAN):
            terms[stage, b * rank:(b + 1) * rank] = fisher[:, b * LANES:(b + 1) * LANES]

        def give(q):
            k = stage * PLANE + q
            j = ls[q // NY] + ys[q % NY]
            to = p * PLANE + j
            unit = 2 * (up_block(p, j) - first)

            @pl.when(is_whole(p, j))
            def _():
                remote(terms.at[stage, rows(unit, 2)], fishers_in.at[rows(2 * k, 2)], f_send, f_recv, (to, r)).start()

            @pl.when(jnp.logical_not(is_whole(p, j)))
            def _():
                remote(terms.at[stage, rows(unit + j % 2, 1)], fishers_in.at[rows(2 * k, 1)], f_send, f_recv, (to, r)).start()

        for q in range(PLANE):
            if q < PLANE - 1:
                give(q)
            else:
                pl.when(stage < NX - 1)(functools.partial(give, q))
        return 0

    lax.fori_loop(0, NX, up_stage, 0)

    down_stage()

    j = c % PLANE
    whole = is_whole(x, j)
    unit = 2 * (up_block(x, j) - first_block(x))

    @pl.when(whole)
    def _():
        own[0] = terms[NX - 1, rows(unit, 2)]
        own[1] = adapt[:, lanes(up_block(x, j))]

    @pl.when(jnp.logical_not(whole))
    def _():
        block = down_block(x, j)
        own[0, :half] = terms[NX - 1, rows(unit + j % 2, 1)]
        own[0, half:] = dterms[rows(2 * block + j % 2, 1)]
        own[1, :half] = adapt[rows(j % 2, 1), lanes(up_block(x, j))]
        own[1, half:] = adapt[rows(j % 2, 1), lanes(wc // LANES + block)]

    remote(factors, factors, a_send, a_recv, other).wait_recv()
    remote(fishers_in, fishers_in, f_send, f_recv, other).wait_recv()
    total = own[0].astype(F32)
    weighted = total * own[1].astype(F32)

    def add(k, sums):
        fisher = fishers_in[rows(2 * k, 2)].astype(F32)
        return sums[0] + fisher, sums[1] + fisher * factors[rows(2 * k, 2)].astype(F32)

    total, weighted = lax.fori_loop(0, OWNERS - 1, add, (total, weighted), unroll=True)
    merged[...] = (weighted / (total + EPS)).astype(BF16)

    def publish(k, _):
        remote(merged, gathered.at[rows(2 * c, 2)], out_send, out_recv, (target(k), r)).start()
        return 0

    for k in range(OWNERS - 1):
        publish(k, 0)
    gathered[rows(2 * c, 2)] = merged[...]

    for step in range(steps):
        exchange(step).wait_send()
        broadcast_all(step).wait_send()
    for kind in (PROJECTED, PULLED):
        token_swap(kind).wait_send()
    remote(factors, factors, a_send, a_recv, other).wait_send()
    remote(fishers_in, fishers_in, f_send, f_recv, other).wait_send()
    ref = gathered.at[pl.ds(0, rank * (OWNERS - 1))]
    remote(ref, ref, out_send, out_recv, other).wait()
    for owner in range(OWNERS):
        p, j = owner // PLANE, owner % PLANE
        h = j % 2
        if j < (6 if p < NX - 1 else 4):
            block = SPAN * p + j
            out[:, block * LANES:(block + 1) * LANES] = gathered[owner * rank:(owner + 1) * rank]
        else:
            block, dblock = (SPAN * p + 6, p) if p < NX - 1 else (25 + (j - 4) // 2, 3 + (j - 4) // 2)
            dblock += wc // LANES
            out[h * half:(h + 1) * half, block * LANES:(block + 1) * LANES] = gathered[owner * rank:owner * rank + half]
            out[h * half:(h + 1) * half, dblock * LANES:(dblock + 1) * LANES] = gathered[owner * rank + half:(owner + 1) * rank]


def local(*args):
    activations, cotangent, lengths, adapter_down, adapter_up = args
    _, seqs, span, wa = activations.shape
    wc = cotangent.shape[3]
    rank = adapter_down.shape[1]
    half = rank // 2
    width = wa + wc
    dma = pltpu.SemaphoreType.DMA
    out = pl.pallas_call(
        kernel,
        out_shape=jax.ShapeDtypeStruct((rank, width), BF16),
        in_specs=[pl.BlockSpec(memory_space=pl.ANY)] * 5,
        out_specs=pl.BlockSpec(memory_space=pltpu.VMEM),
        scratch_shapes=[
            pltpu.VMEM((seqs, span, width), BF16),
            pltpu.VMEM((rank, width), BF16),
            pltpu.SMEM((1, seqs), jnp.int32),
            pltpu.VMEM((2, 2, seqs, half, span), F32),
            pltpu.VMEM((2, seqs, half, span), F32),
            pltpu.VMEM((2, seqs, half, span), BF16),
            pltpu.VMEM((2, NH - 1, seqs, half, span), BF16),
            pltpu.VMEM((2, 2, seqs, half, span), BF16),
            pltpu.VMEM((NX, SPAN * rank, LANES), BF16),
            pltpu.VMEM((wa // LANES * rank, LANES), BF16),
            pltpu.VMEM((rank * (OWNERS - 1), LANES), BF16),
            pltpu.VMEM((rank * (OWNERS - 1), LANES), BF16),
            pltpu.VMEM((2, rank, LANES), BF16),
            pltpu.VMEM((rank, LANES), BF16),
            pltpu.VMEM((rank * OWNERS, LANES), BF16),
            dma((seqs + 1,)), dma((3,)), dma((3,)), dma((3,)), dma((3,)), dma((3,)), dma((2,)), dma((2,)),
            dma, dma, dma, dma, dma, dma, pltpu.SemaphoreType.REGULAR, pltpu.SemaphoreType.REGULAR,
        ],
        compiler_params=pltpu.CompilerParams(
            collective_id=0, has_side_effects=True, vmem_limit_bytes=48 * 1024 * 1024
        ),
    )(*(pltpu.with_memory_space_constraint(a, pltpu.HBM) for a in args))
    return out[:, wc:], out[:, :wc]


def solution(mesh):
    in_specs = (
        P("client", None, None, "row"),
        P("client", None, None, "row"),
        P("client", None),
        P("client", None, "row"),
        P("client", None, "row"),
    )
    out_specs = (P(None, "row"), P(None, "row"))
    return jax.shard_map(local, mesh=mesh, in_specs=in_specs, out_specs=out_specs, check_vma=False)
```

```python
import functools

import functools

import jax
import jax.numpy as jnp
from jax import lax
from jax.experimental import pallas as pl
from jax.experimental.pallas import tpu as pltpu
from jax.sharding import PartitionSpec as P

EPS = 1e-06
MESH = pl.DeviceIdType.MESH
LANES = 128
F32 = jnp.float32
BF16 = jnp.bfloat16
NT = (((1,), (1,)), ((), ()))
NX, NL, NY = 4, 2, 4
NH, NCORE = 4, 2
PLANE = NL * NY
OWNERS = NX * PLANE
UP_BLOCKS = 27
SPAN = 7
PROJECTED, PULLED = 0, 1
FINISH_AT = 2
SPLITS = (2, 2)
FIRST = 3


def hops(offset):
    return sum(min(d, n - d) for d, n in zip(offset, (NX, NL, NY)))


def pick(v, a, b, c, d):
    return jnp.where(v == 0, a, jnp.where(v == 1, b, jnp.where(v == 2, c, d)))


def kernel(
    act, cot, lens, down, up, out,
    data, adapt, lens_s, part, sibling, pair, arrived, tokens, terms, dterms, factors, fishers_in, own, merged, gathered,
    load_sem, small_sem, ex_send, ex_recv, bc_send, bc_recv, tk_send, tk_recv,
    a_send, a_recv, f_send, f_recv, out_send, out_recv, plane_sem, all_sem,
):
    seqs, span, wa = act.shape[1:]
    wc = cot.shape[3]
    rank = down.shape[1]
    half = rank // 2
    c = lax.axis_index("client")
    r = lax.axis_index("row")
    x, lo, y = c // PLANE, (c // NY) % NL, c % NY
    hi, core = r // NCORE, r % NCORE

    def client(dx, dl, dy):
        return lax.rem(x + dx, NX) * PLANE + lax.rem(lo + dl, NL) * NY + lax.rem(y + dy, NY)

    def chip(k):
        return (c, lax.rem(hi + k, NH) * NCORE + core)

    xs = [lax.rem(x + d, NX) * PLANE for d in (2, 1, 3, 0)]
    ls = [lax.rem(lo + d, NL) * NY for d in (1, 0)]
    ys = [lax.rem(y + d, NY) for d in (2, 1, 3, 0)]

    def target(k):
        if isinstance(k, int):
            return xs[k // PLANE] + ls[k % PLANE // NY] + ys[k % NY]
        v, q = k // PLANE, k % PLANE
        return client(pick(v, 2, 1, 3, 0), 1 - q // NY, pick(q % NY, 2, 1, 3, 0))

    def slot_at(to):
        dx, dl, dy = lax.rem(to // PLANE - x + NX, NX), lax.rem(to // NY % NL - lo + NL, NL), lax.rem(to % NY - y + NY, NY)
        return pick(dx, 3, 1, 0, 2) * PLANE + (1 - dl) * NY + pick(dy, 3, 1, 0, 2)

    def rows(unit, n):
        return pl.ds(pl.multiple_of(unit * half, half), n * half)

    def lanes(block):
        return pl.ds(pl.multiple_of(block * LANES, LANES), LANES)

    def is_whole(p, j):
        return j < jnp.where(p < NX - 1, 6, 4)

    def up_block(p, j):
        return jnp.where(p < NX - 1, p * SPAN + jnp.minimum(j, SPAN - 1), jnp.where(j < 4, 21 + j, 25 + (j - 4) // 2))

    def down_block(p, j):
        return jnp.where(p < NX - 1, p, 3 + (j - 4) // 2)

    def first_block(p):
        return jnp.minimum(p * SPAN, UP_BLOCKS - SPAN)

    other = (c, hi * NCORE + 1 - core)
    peers = [other] + [chip(k) for k in (2, 1, 3)]
    along_y = [(client(0, 0, k), r) for k in (2, 1, 3)]
    peers += [(client(k, 0, 0), r) for k in (2, 1, 3)] + along_y + [(client(0, 1, 0), r)]

    small = [
        pltpu.make_async_copy(down.at[0], adapt.at[:, pl.ds(wc, wa)], small_sem.at[0]),
        pltpu.make_async_copy(up.at[0], adapt.at[:, pl.ds(0, wc)], small_sem.at[1]),
        pltpu.make_async_copy(lens, lens_s, small_sem.at[2]),
    ]
    load_act = pltpu.make_async_copy(act.at[0], data.at[:, :, pl.ds(wc, wa)], load_sem.at[seqs])

    def load_cot(e):
        return pltpu.make_async_copy(cot.at[0, e], data.at[e, :, pl.ds(0, wc)], load_sem.at[e])

    loads = [small[0], load_act, small[1]] + [load_cot(e) for e in range(seqs)] + [small[2]]
    for copy in loads[:FIRST]:
        copy.start()

    barrier = pltpu.get_barrier_semaphore()
    for peer in peers:
        pl.semaphore_signal(barrier, inc=1, device_id=peer, device_id_type=MESH)
    for copy in loads[FIRST:]:
        copy.start()

    def remote(src, dst, send, recv, to):
        return pltpu.make_async_remote_copy(
            src_ref=src, dst_ref=dst, send_sem=send, recv_sem=recv, device_id=to, device_id_type=MESH
        )

    ends = [sum(SPLITS[:i + 1]) for i in range(len(SPLITS))]
    steps = 1 + len(SPLITS)

    def piece(step):
        return (PROJECTED, pl.ds(0, seqs)) if step == 0 else (PULLED, pl.ds(ends[step - 1] - SPLITS[step - 1], SPLITS[step - 1]))

    def exchange(step):
        kind, which = piece(step)
        return remote(part.at[kind, 1 - core, which], sibling.at[kind, which], ex_send.at[step], ex_recv.at[step], other)

    def broadcast(step):
        kind, which = piece(step)
        exchange(step).wait_recv()
        pair[kind, which] = (part[kind, core, which] + sibling[kind, which]).astype(BF16)
        for k in (2, 1, 3):
            remote(pair.at[kind, which], arrived.at[kind, k - 1, which], bc_send.at[step], bc_recv.at[step], chip(k)).start()

    def broadcast_all(step):
        kind, which = piece(step)
        ref = arrived.at[kind, :, which]
        return remote(ref, ref, bc_send.at[step], bc_recv.at[step], other)

    def token_swap(kind):
        ref = tokens.at[kind, core]
        return remote(ref, ref, tk_send.at[kind], tk_recv.at[kind], other)

    def finish(kind):
        for step in ((0,) if kind == PROJECTED else range(1, steps)):
            broadcast_all(step).wait_recv()
        position = lax.broadcasted_iota(jnp.int32, (1, span), 1)
        for e in range(seqs):
            total = part[kind, core, e] + sibling[kind, e]
            for k in range(NH - 1):
                total += arrived[kind, k, e].astype(F32)
            length = jnp.full((1, span), lens_s[0, e], jnp.int32)
            weight = (position < length).astype(F32) / length.astype(F32)
            tokens[kind, core, e] = (total * weight).astype(BF16)
        token_swap(kind).start()

    def meet():
        pl.semaphore_wait(barrier, len(peers))
        exchange(0).start()
        for peer in along_y:
            pl.semaphore_signal(plane_sem, inc=1, device_id=peer, device_id_type=MESH)

    load_act.wait()
    small[0].wait()
    for e in range(seqs):
        projected = lax.dot_general(adapt[:, wc:], data[e, :, wc:], NT, preferred_element_type=F32)
        part[PROJECTED, 0, e] = projected[:half]
        part[PROJECTED, 1, e] = projected[half:]
    small[1].wait()

    def pull(e, _):
        load_cot(e).wait()
        pulled = lax.dot_general(adapt[:, :wc], data[e, :, :wc], NT, preferred_element_type=F32)
        part[PULLED, 0, e] = pulled[:half]
        part[PULLED, 1, e] = pulled[half:]

        pl.when(e == 0)(meet)

        for step in range(1, steps):
            pl.when(e == sent_at[step])(exchange(step).start)
        for step in range(steps):
            if cast_at[step] < seqs:
                pl.when(e == cast_at[step])(functools.partial(broadcast, step))
        return 0

    sent_at = [0] + [end - 1 for end in ends]
    cast_at = [0] + [end for end in ends]
    lax.fori_loop(0, seqs, pull, 0)
    for step in range(steps):
        if cast_at[step] >= seqs:
            broadcast(step)
    pl.semaphore_wait(plane_sem, NY - 1)
    pl.semaphore_signal(all_sem, inc=1, device_id=(client(0, 1, 0), r), device_id_type=MESH)
    small[2].wait()

    def give_factors(v, _):
        p = lax.rem(x + pick(v, 2, 1, 3, 0), NX)
        for q in range(PLANE):
            if q < PLANE - 1:
                give_factor(v, p, q)
            else:
                pl.when(v < NX - 1)(functools.partial(give_factor, v, p, q))
        return 0

    def give_factor(v, p, q):
        k = v * PLANE + q
        j = ls[q // NY] + ys[q % NY]
        to = p * PLANE + j
        block, h = up_block(p, j), j % 2

        @pl.when(is_whole(p, j))
        def _():
            remote(adapt.at[:, lanes(block)], factors.at[rows(2 * k, 2)], a_send, a_recv, (to, r)).start()

        @pl.when(jnp.logical_not(is_whole(p, j)))
        def _():
            remote(adapt.at[rows(h, 1), lanes(block)], factors.at[rows(2 * k, 1)], a_send, a_recv, (to, r)).start()
            block2 = wc // LANES + down_block(p, j)
            remote(adapt.at[rows(h, 1), lanes(block2)], factors.at[rows(2 * k + 1, 1)], a_send, a_recv, (to, r)).start()


    pl.semaphore_wait(all_sem, 1)
    lax.fori_loop(0, NX, give_factors, 0)
    finish(PROJECTED)

    def fishers(kind, columns, width):
        total = jnp.zeros((rank, width), F32)
        for e in range(seqs):
            left = jnp.concatenate([tokens[kind, 0, e], tokens[kind, 1, e]], axis=0)
            grad = jnp.dot(left, data[e, :, columns], preferred_element_type=F32)
            total += grad * grad
        return total.astype(BF16)

    token_swap(PROJECTED).wait_recv()

    units = 2 * (wa // LANES)

    def down_stage():
        token_swap(PULLED).wait_recv()
        fisher = fishers(PULLED, pl.ds(wc, wa), wa)
        for b in range(wa // LANES):
            dterms[b * rank:(b + 1) * rank] = fisher[:, b * LANES:(b + 1) * LANES]

        def give_down(k, _):
            n = lax.rem(c + k, units)
            to = jnp.minimum(n // 2, NX - 1) * PLANE + jnp.where(n < 6, 6 + n % 2, n - 2)

            @pl.when(c != to)
            def _():
                remote(dterms.at[rows(n, 1)], fishers_in.at[rows(2 * slot_at(to) + 1, 1)], f_send, f_recv, (to, r)).start()

            return 0

        lax.fori_loop(0, units, give_down, 0)

    def up_stage(stage, _):
        @pl.when(stage == FINISH_AT)
        def _():
            finish(PULLED)

        p = lax.rem(x + pick(stage, 2, 1, 3, 0), NX)
        first = first_block(p)
        fisher = fishers(PROJECTED, pl.ds(pl.multiple_of(first * LANES, LANES), SPAN * LANES), SPAN * LANES)
        for b in range(SPAN):
            terms[stage, b * rank:(b + 1) * rank] = fisher[:, b * LANES:(b + 1) * LANES]

        def give(q):
            k = stage * PLANE + q
            j = ls[q // NY] + ys[q % NY]
            to = p * PLANE + j
            unit = 2 * (up_block(p, j) - first)

            @pl.when(is_whole(p, j))
            def _():
                remote(terms.at[stage, rows(unit, 2)], fishers_in.at[rows(2 * k, 2)], f_send, f_recv, (to, r)).start()

            @pl.when(jnp.logical_not(is_whole(p, j)))
            def _():
                remote(terms.at[stage, rows(unit + j % 2, 1)], fishers_in.at[rows(2 * k, 1)], f_send, f_recv, (to, r)).start()

        for q in range(PLANE):
            if q < PLANE - 1:
                give(q)
            else:
                pl.when(stage < NX - 1)(functools.partial(give, q))
        return 0

    lax.fori_loop(0, NX, up_stage, 0)

    down_stage()

    j = c % PLANE
    whole = is_whole(x, j)
    unit = 2 * (up_block(x, j) - first_block(x))

    @pl.when(whole)
    def _():
        own[0] = terms[NX - 1, rows(unit, 2)]
        own[1] = adapt[:, lanes(up_block(x, j))]

    @pl.when(jnp.logical_not(whole))
    def _():
        block = down_block(x, j)
        own[0, :half] = terms[NX - 1, rows(unit + j % 2, 1)]
        own[0, half:] = dterms[rows(2 * block + j % 2, 1)]
        own[1, :half] = adapt[rows(j % 2, 1), lanes(up_block(x, j))]
        own[1, half:] = adapt[rows(j % 2, 1), lanes(wc // LANES + block)]

    remote(factors, factors, a_send, a_recv, other).wait_recv()
    remote(fishers_in, fishers_in, f_send, f_recv, other).wait_recv()
    total = own[0].astype(F32)
    weighted = total * own[1].astype(F32)

    def add(k, sums):
        fisher = fishers_in[rows(2 * k, 2)].astype(F32)
        return sums[0] + fisher, sums[1] + fisher * factors[rows(2 * k, 2)].astype(F32)

    total, weighted = lax.fori_loop(0, OWNERS - 1, add, (total, weighted), unroll=True)
    merged[...] = (weighted / (total + EPS)).astype(BF16)

    def publish(to):
        remote(merged, gathered.at[rows(2 * c, 2)], out_send, out_recv, (to, r)).start()

    offsets = [(dx, dl, dy) for dx in range(NX) for dl in range(NL) for dy in range(NY)][1:]
    for offset in sorted(offsets, key=lambda o: (-hops(o), (o[0] + o[2]) % 4, o[1])):
        publish(client(*offset))
    gathered[rows(2 * c, 2)] = merged[...]

    for step in range(steps):
        exchange(step).wait_send()
        broadcast_all(step).wait_send()
    for kind in (PROJECTED, PULLED):
        token_swap(kind).wait_send()
    remote(factors, factors, a_send, a_recv, other).wait_send()
    remote(fishers_in, fishers_in, f_send, f_recv, other).wait_send()
    ref = gathered.at[pl.ds(0, rank * (OWNERS - 1))]
    remote(ref, ref, out_send, out_recv, other).wait()
    for owner in range(OWNERS):
        p, j = owner // PLANE, owner % PLANE
        h = j % 2
        if j < (6 if p < NX - 1 else 4):
            block = SPAN * p + j
            out[:, block * LANES:(block + 1) * LANES] = gathered[owner * rank:(owner + 1) * rank]
        else:
            block, dblock = (SPAN * p + 6, p) if p < NX - 1 else (25 + (j - 4) // 2, 3 + (j - 4) // 2)
            dblock += wc // LANES
            out[h * half:(h + 1) * half, block * LANES:(block + 1) * LANES] = gathered[owner * rank:owner * rank + half]
            out[h * half:(h + 1) * half, dblock * LANES:(dblock + 1) * LANES] = gathered[owner * rank + half:(owner + 1) * rank]


def local(*args):
    activations, cotangent, lengths, adapter_down, adapter_up = args
    _, seqs, span, wa = activations.shape
    wc = cotangent.shape[3]
    rank = adapter_down.shape[1]
    half = rank // 2
    width = wa + wc
    dma = pltpu.SemaphoreType.DMA
    out = pl.pallas_call(
        kernel,
        out_shape=jax.ShapeDtypeStruct((rank, width), BF16),
        in_specs=[pl.BlockSpec(memory_space=pl.ANY)] * 5,
        out_specs=pl.BlockSpec(memory_space=pltpu.VMEM),
        scratch_shapes=[
            pltpu.VMEM((seqs, span, width), BF16),
            pltpu.VMEM((rank, width), BF16),
            pltpu.SMEM((1, seqs), jnp.int32),
            pltpu.VMEM((2, 2, seqs, half, span), F32),
            pltpu.VMEM((2, seqs, half, span), F32),
            pltpu.VMEM((2, seqs, half, span), BF16),
            pltpu.VMEM((2, NH - 1, seqs, half, span), BF16),
            pltpu.VMEM((2, 2, seqs, half, span), BF16),
            pltpu.VMEM((NX, SPAN * rank, LANES), BF16),
            pltpu.VMEM((wa // LANES * rank, LANES), BF16),
            pltpu.VMEM((rank * (OWNERS - 1), LANES), BF16),
            pltpu.VMEM((rank * (OWNERS - 1), LANES), BF16),
            pltpu.VMEM((2, rank, LANES), BF16),
            pltpu.VMEM((rank, LANES), BF16),
            pltpu.VMEM((rank * OWNERS, LANES), BF16),
            dma((seqs + 1,)), dma((3,)), dma((3,)), dma((3,)), dma((3,)), dma((3,)), dma((2,)), dma((2,)),
            dma, dma, dma, dma, dma, dma, pltpu.SemaphoreType.REGULAR, pltpu.SemaphoreType.REGULAR,
        ],
        compiler_params=pltpu.CompilerParams(
            collective_id=0, has_side_effects=True, vmem_limit_bytes=48 * 1024 * 1024
        ),
    )(*(pltpu.with_memory_space_constraint(a, pltpu.HBM) for a in args))
    return out[:, wc:], out[:, :wc]


def solution(mesh):
    in_specs = (
        P("client", None, None, "row"),
        P("client", None, None, "row"),
        P("client", None),
        P("client", None, "row"),
        P("client", None, "row"),
    )
    out_specs = (P(None, "row"), P(None, "row"))
    return jax.shard_map(local, mesh=mesh, in_specs=in_specs, out_specs=out_specs, check_vma=False)
```

```python
import functools

import functools

import jax
import jax.numpy as jnp
from jax import lax
from jax.experimental import pallas as pl
from jax.experimental.pallas import tpu as pltpu
from jax.sharding import PartitionSpec as P

EPS = 1e-06
MESH = pl.DeviceIdType.MESH
LANES = 128
F32 = jnp.float32
BF16 = jnp.bfloat16
NT = (((1,), (1,)), ((), ()))
NX, NL, NY = 4, 2, 4
NH, NCORE = 4, 2
PLANE = NL * NY
OWNERS = NX * PLANE
UP_BLOCKS = 27
SPAN = 7
PROJECTED, PULLED = 0, 1
FINISH_AT = 2
SPLITS = (2, 2)
FIRST = 3


def hops(offset):
    return sum(min(d, n - d) for d, n in zip(offset, (NX, NL, NY)))


def pick(v, a, b, c, d):
    return jnp.where(v == 0, a, jnp.where(v == 1, b, jnp.where(v == 2, c, d)))


def kernel(
    act, cot, lens, down, up, out,
    data, adapt, lens_s, part, sibling, pair, arrived, tokens, terms, dterms, factors, fishers_in, own, merged, gathered,
    load_sem, small_sem, ex_send, ex_recv, bc_send, bc_recv, tk_send, tk_recv,
    a_send, a_recv, f_send, f_recv, out_send, out_recv, plane_sem, all_sem,
):
    seqs, span, wa = act.shape[1:]
    wc = cot.shape[3]
    rank = down.shape[1]
    half = rank // 2
    c = lax.axis_index("client")
    r = lax.axis_index("row")
    x, lo, y = c // PLANE, (c // NY) % NL, c % NY
    hi, core = r // NCORE, r % NCORE

    def client(dx, dl, dy):
        return lax.rem(x + dx, NX) * PLANE + lax.rem(lo + dl, NL) * NY + lax.rem(y + dy, NY)

    def chip(k):
        return (c, lax.rem(hi + k, NH) * NCORE + core)

    xs = [lax.rem(x + d, NX) * PLANE for d in (2, 1, 3, 0)]
    ls = [lax.rem(lo + d, NL) * NY for d in (1, 0)]
    ys = [lax.rem(y + d, NY) for d in (2, 1, 3, 0)]

    def target(k):
        if isinstance(k, int):
            return xs[k // PLANE] + ls[k % PLANE // NY] + ys[k % NY]
        v, q = k // PLANE, k % PLANE
        return client(pick(v, 2, 1, 3, 0), 1 - q // NY, pick(q % NY, 2, 1, 3, 0))

    def slot_at(to):
        dx, dl, dy = lax.rem(to // PLANE - x + NX, NX), lax.rem(to // NY % NL - lo + NL, NL), lax.rem(to % NY - y + NY, NY)
        return pick(dx, 3, 1, 0, 2) * PLANE + (1 - dl) * NY + pick(dy, 3, 1, 0, 2)

    def rows(unit, n):
        return pl.ds(pl.multiple_of(unit * half, half), n * half)

    def lanes(block):
        return pl.ds(pl.multiple_of(block * LANES, LANES), LANES)

    def is_whole(p, j):
        return j < jnp.where(p < NX - 1, 6, 4)

    def up_block(p, j):
        return jnp.where(p < NX - 1, p * SPAN + jnp.minimum(j, SPAN - 1), jnp.where(j < 4, 21 + j, 25 + (j - 4) // 2))

    def down_block(p, j):
        return jnp.where(p < NX - 1, p, 3 + (j - 4) // 2)

    def first_block(p):
        return jnp.minimum(p * SPAN, UP_BLOCKS - SPAN)

    other = (c, hi * NCORE + 1 - core)
    peers = [other] + [chip(k) for k in (2, 1, 3)]
    along_y = [(client(0, 0, k), r) for k in (2, 1, 3)]
    peers += [(client(k, 0, 0), r) for k in (2, 1, 3)] + along_y + [(client(0, 1, 0), r)]

    small = [
        pltpu.make_async_copy(down.at[0], adapt.at[:, pl.ds(wc, wa)], small_sem.at[0]),
        pltpu.make_async_copy(up.at[0], adapt.at[:, pl.ds(0, wc)], small_sem.at[1]),
        pltpu.make_async_copy(lens, lens_s, small_sem.at[2]),
    ]
    load_act = pltpu.make_async_copy(act.at[0], data.at[:, :, pl.ds(wc, wa)], load_sem.at[seqs])

    def load_cot(e):
        return pltpu.make_async_copy(cot.at[0, e], data.at[e, :, pl.ds(0, wc)], load_sem.at[e])

    loads = [small[0], load_act, small[1]] + [load_cot(e) for e in range(seqs)] + [small[2]]
    for copy in loads[:FIRST]:
        copy.start()

    barrier = pltpu.get_barrier_semaphore()
    for peer in peers:
        pl.semaphore_signal(barrier, inc=1, device_id=peer, device_id_type=MESH)
    for copy in loads[FIRST:]:
        copy.start()

    def remote(src, dst, send, recv, to):
        return pltpu.make_async_remote_copy(
            src_ref=src, dst_ref=dst, send_sem=send, recv_sem=recv, device_id=to, device_id_type=MESH
        )

    ends = [sum(SPLITS[:i + 1]) for i in range(len(SPLITS))]
    steps = 1 + len(SPLITS)

    def piece(step):
        return (PROJECTED, pl.ds(0, seqs)) if step == 0 else (PULLED, pl.ds(ends[step - 1] - SPLITS[step - 1], SPLITS[step - 1]))

    def exchange(step):
        kind, which = piece(step)
        return remote(part.at[kind, 1 - core, which], sibling.at[kind, which], ex_send.at[step], ex_recv.at[step], other)

    def broadcast(step):
        kind, which = piece(step)
        exchange(step).wait_recv()
        pair[kind, which] = (part[kind, core, which] + sibling[kind, which]).astype(BF16)
        for k in (2, 1, 3):
            remote(pair.at[kind, which], arrived.at[kind, k - 1, which], bc_send.at[step], bc_recv.at[step], chip(k)).start()

    def broadcast_all(step):
        kind, which = piece(step)
        ref = arrived.at[kind, :, which]
        return remote(ref, ref, bc_send.at[step], bc_recv.at[step], other)

    def token_swap(kind):
        ref = tokens.at[kind, core]
        return remote(ref, ref, tk_send.at[kind], tk_recv.at[kind], other)

    def finish(kind):
        for step in ((0,) if kind == PROJECTED else range(1, steps)):
            broadcast_all(step).wait_recv()
        position = lax.broadcasted_iota(jnp.int32, (1, span), 1)
        for e in range(seqs):
            total = part[kind, core, e] + sibling[kind, e]
            for k in range(NH - 1):
                total += arrived[kind, k, e].astype(F32)
            length = jnp.full((1, span), lens_s[0, e], jnp.int32)
            weight = (position < length).astype(F32) / length.astype(F32)
            tokens[kind, core, e] = (total * weight).astype(BF16)
        token_swap(kind).start()

    def meet():
        pl.semaphore_wait(barrier, len(peers))
        exchange(0).start()
        for peer in along_y:
            pl.semaphore_signal(plane_sem, inc=1, device_id=peer, device_id_type=MESH)

    load_act.wait()
    small[0].wait()
    for e in range(seqs):
        projected = lax.dot_general(adapt[:, wc:], data[e, :, wc:], NT, preferred_element_type=F32)
        part[PROJECTED, 0, e] = projected[:half]
        part[PROJECTED, 1, e] = projected[half:]
    small[1].wait()

    def pull(e, _):
        load_cot(e).wait()
        pulled = lax.dot_general(adapt[:, :wc], data[e, :, :wc], NT, preferred_element_type=F32)
        part[PULLED, 0, e] = pulled[:half]
        part[PULLED, 1, e] = pulled[half:]

        pl.when(e == 0)(meet)

        for step in range(1, steps):
            pl.when(e == sent_at[step])(exchange(step).start)
        for step in range(steps):
            if cast_at[step] < seqs:
                pl.when(e == cast_at[step])(functools.partial(broadcast, step))
        return 0

    sent_at = [0] + [end - 1 for end in ends]
    cast_at = [0] + [end for end in ends]
    lax.fori_loop(0, seqs, pull, 0)
    for step in range(steps):
        if cast_at[step] >= seqs:
            broadcast(step)
    pl.semaphore_wait(plane_sem, NY - 1)
    pl.semaphore_signal(all_sem, inc=1, device_id=(client(0, 1, 0), r), device_id_type=MESH)
    small[2].wait()

    def give_factors(v, _):
        p = lax.rem(x + pick(v, 2, 1, 3, 0), NX)
        for q in range(PLANE):
            if q < PLANE - 1:
                give_factor(v, p, q)
            else:
                pl.when(v < NX - 1)(functools.partial(give_factor, v, p, q))
        return 0

    def give_factor(v, p, q):
        k = v * PLANE + q
        j = ls[q // NY] + ys[q % NY]
        to = p * PLANE + j
        block, h = up_block(p, j), j % 2

        @pl.when(is_whole(p, j))
        def _():
            remote(adapt.at[:, lanes(block)], factors.at[rows(2 * k, 2)], a_send, a_recv, (to, r)).start()

        @pl.when(jnp.logical_not(is_whole(p, j)))
        def _():
            remote(adapt.at[rows(h, 1), lanes(block)], factors.at[rows(2 * k, 1)], a_send, a_recv, (to, r)).start()
            block2 = wc // LANES + down_block(p, j)
            remote(adapt.at[rows(h, 1), lanes(block2)], factors.at[rows(2 * k + 1, 1)], a_send, a_recv, (to, r)).start()


    pl.semaphore_wait(all_sem, 1)
    lax.fori_loop(0, NX, give_factors, 0)
    finish(PROJECTED)

    def fishers(kind, columns, width):
        total = jnp.zeros((rank, width), F32)
        for e in range(seqs):
            left = jnp.concatenate([tokens[kind, 0, e], tokens[kind, 1, e]], axis=0)
            grad = jnp.dot(left, data[e, :, columns], preferred_element_type=F32)
            total += grad * grad
        return total.astype(BF16)

    token_swap(PROJECTED).wait_recv()

    units = 2 * (wa // LANES)

    def down_stage():
        token_swap(PULLED).wait_recv()
        fisher = fishers(PULLED, pl.ds(wc, wa), wa)
        for b in range(wa // LANES):
            dterms[b * rank:(b + 1) * rank] = fisher[:, b * LANES:(b + 1) * LANES]

        def give_down(k, _):
            n = lax.rem(c + k, units)
            to = jnp.minimum(n // 2, NX - 1) * PLANE + jnp.where(n < 6, 6 + n % 2, n - 2)

            @pl.when(c != to)
            def _():
                remote(dterms.at[rows(n, 1)], fishers_in.at[rows(2 * slot_at(to) + 1, 1)], f_send, f_recv.at[1], (to, r)).start()

            return 0

        lax.fori_loop(0, units, give_down, 0)

    def up_stage(stage, _):
        @pl.when(stage == FINISH_AT)
        def _():
            finish(PULLED)

        p = lax.rem(x + pick(stage, 2, 1, 3, 0), NX)
        first = first_block(p)
        fisher = fishers(PROJECTED, pl.ds(pl.multiple_of(first * LANES, LANES), SPAN * LANES), SPAN * LANES)
        for b in range(SPAN):
            terms[stage, b * rank:(b + 1) * rank] = fisher[:, b * LANES:(b + 1) * LANES]

        def give(q):
            k = stage * PLANE + q
            j = ls[q // NY] + ys[q % NY]
            to = p * PLANE + j
            unit = 2 * (up_block(p, j) - first)

            @pl.when(is_whole(p, j))
            def _():
                remote(terms.at[stage, rows(unit, 2)], fishers_in.at[rows(2 * k, 2)], f_send, f_recv.at[stage // (NX - 1)], (to, r)).start()

            @pl.when(jnp.logical_not(is_whole(p, j)))
            def _():
                remote(terms.at[stage, rows(unit + j % 2, 1)], fishers_in.at[rows(2 * k, 1)], f_send, f_recv.at[stage // (NX - 1)], (to, r)).start()

        for q in range(PLANE):
            if q < PLANE - 1:
                give(q)
            else:
                pl.when(stage < NX - 1)(functools.partial(give, q))
        return 0

    lax.fori_loop(0, NX, up_stage, 0)

    down_stage()

    j = c % PLANE
    whole = is_whole(x, j)
    unit = 2 * (up_block(x, j) - first_block(x))

    @pl.when(whole)
    def _():
        own[0] = terms[NX - 1, rows(unit, 2)]
        own[1] = adapt[:, lanes(up_block(x, j))]

    @pl.when(jnp.logical_not(whole))
    def _():
        block = down_block(x, j)
        own[0, :half] = terms[NX - 1, rows(unit + j % 2, 1)]
        own[0, half:] = dterms[rows(2 * block + j % 2, 1)]
        own[1, :half] = adapt[rows(j % 2, 1), lanes(up_block(x, j))]
        own[1, half:] = adapt[rows(j % 2, 1), lanes(wc // LANES + block)]

    remote(factors, factors, a_send, a_recv, other).wait_recv()
    early = PLANE * (NX - 1)

    def await_units(n, which):
        ref = fishers_in.at[pl.ds(0, n * half)]
        remote(ref, ref, f_send, f_recv.at[which], other).wait_recv()

    def sums(at, start, stop, n):
        total = own[0, at:at + n].astype(F32)
        return add(total, total * own[1, at:at + n].astype(F32), at, start, stop, n)

    def add(total, weighted, at, start, stop, n):
        for k in range(start, stop):
            here = pl.ds(k * rank + at, n)
            fisher = fishers_in[here].astype(F32)
            total += fisher
            weighted += fisher * factors[here].astype(F32)
        return total, weighted

    pl.when(whole)(functools.partial(await_units, 2 * early, 0))
    pl.when(jnp.logical_not(whole))(functools.partial(await_units, early, 0))
    top = sums(0, 0, early, half)
    pl.when(whole)(functools.partial(await_units, 2 * (OWNERS - 1 - early), 1))
    pl.when(jnp.logical_not(whole))(functools.partial(await_units, 2 * (OWNERS - 1) - early, 1))
    top = add(*top, 0, early, OWNERS - 1, half)
    bottom = sums(half, 0, OWNERS - 1, half)
    total, weighted = (jnp.concatenate(pair_of, axis=0) for pair_of in zip(top, bottom))
    merged[...] = (weighted / (total + EPS)).astype(BF16)

    def publish(to):
        remote(merged, gathered.at[rows(2 * c, 2)], out_send, out_recv, (to, r)).start()

    offsets = [(dx, dl, dy) for dx in range(NX) for dl in range(NL) for dy in range(NY)][1:]
    for offset in sorted(offsets, key=lambda o: (-hops(o), (o[0] + o[2]) % 4, o[1])):
        publish(client(*offset))
    gathered[rows(2 * c, 2)] = merged[...]

    for step in range(steps):
        exchange(step).wait_send()
        broadcast_all(step).wait_send()
    for kind in (PROJECTED, PULLED):
        token_swap(kind).wait_send()
    remote(factors, factors, a_send, a_recv, other).wait_send()
    remote(fishers_in, fishers_in, f_send, f_recv.at[0], other).wait_send()
    ref = gathered.at[pl.ds(0, rank * (OWNERS - 1))]
    remote(ref, ref, out_send, out_recv, other).wait()
    for owner in range(OWNERS):
        p, j = owner // PLANE, owner % PLANE
        h = j % 2
        if j < (6 if p < NX - 1 else 4):
            block = SPAN * p + j
            out[:, block * LANES:(block + 1) * LANES] = gathered[owner * rank:(owner + 1) * rank]
        else:
            block, dblock = (SPAN * p + 6, p) if p < NX - 1 else (25 + (j - 4) // 2, 3 + (j - 4) // 2)
            dblock += wc // LANES
            out[h * half:(h + 1) * half, block * LANES:(block + 1) * LANES] = gathered[owner * rank:owner * rank + half]
            out[h * half:(h + 1) * half, dblock * LANES:(dblock + 1) * LANES] = gathered[owner * rank + half:(owner + 1) * rank]


def local(*args):
    activations, cotangent, lengths, adapter_down, adapter_up = args
    _, seqs, span, wa = activations.shape
    wc = cotangent.shape[3]
    rank = adapter_down.shape[1]
    half = rank // 2
    width = wa + wc
    dma = pltpu.SemaphoreType.DMA
    out = pl.pallas_call(
        kernel,
        out_shape=jax.ShapeDtypeStruct((rank, width), BF16),
        in_specs=[pl.BlockSpec(memory_space=pl.ANY)] * 5,
        out_specs=pl.BlockSpec(memory_space=pltpu.VMEM),
        scratch_shapes=[
            pltpu.VMEM((seqs, span, width), BF16),
            pltpu.VMEM((rank, width), BF16),
            pltpu.SMEM((1, seqs), jnp.int32),
            pltpu.VMEM((2, 2, seqs, half, span), F32),
            pltpu.VMEM((2, seqs, half, span), F32),
            pltpu.VMEM((2, seqs, half, span), BF16),
            pltpu.VMEM((2, NH - 1, seqs, half, span), BF16),
            pltpu.VMEM((2, 2, seqs, half, span), BF16),
            pltpu.VMEM((NX, SPAN * rank, LANES), BF16),
            pltpu.VMEM((wa // LANES * rank, LANES), BF16),
            pltpu.VMEM((rank * (OWNERS - 1), LANES), BF16),
            pltpu.VMEM((rank * (OWNERS - 1), LANES), BF16),
            pltpu.VMEM((2, rank, LANES), BF16),
            pltpu.VMEM((rank, LANES), BF16),
            pltpu.VMEM((rank * OWNERS, LANES), BF16),
            dma((seqs + 1,)), dma((3,)), dma((3,)), dma((3,)), dma((3,)), dma((3,)), dma((2,)), dma((2,)),
            dma, dma, dma, dma((2,)), dma, dma, pltpu.SemaphoreType.REGULAR, pltpu.SemaphoreType.REGULAR,
        ],
        compiler_params=pltpu.CompilerParams(
            collective_id=0, has_side_effects=True, vmem_limit_bytes=48 * 1024 * 1024
        ),
    )(*(pltpu.with_memory_space_constraint(a, pltpu.HBM) for a in args))
    return out[:, wc:], out[:, :wc]


def solution(mesh):
    in_specs = (
        P("client", None, None, "row"),
        P("client", None, None, "row"),
        P("client", None),
        P("client", None, "row"),
        P("client", None, "row"),
    )
    out_specs = (P(None, "row"), P(None, "row"))
    return jax.shard_map(local, mesh=mesh, in_specs=in_specs, out_specs=out_specs, check_vma=False)
```

```python
import functools

import functools

import jax
import jax.numpy as jnp
from jax import lax
from jax.experimental import pallas as pl
from jax.experimental.pallas import tpu as pltpu
from jax.sharding import PartitionSpec as P

EPS = 1e-06
MESH = pl.DeviceIdType.MESH
LANES = 128
F32 = jnp.float32
BF16 = jnp.bfloat16
NT = (((1,), (1,)), ((), ()))
NX, NL, NY = 4, 2, 4
NH, NCORE = 4, 2
PLANE = NL * NY
OWNERS = NX * PLANE
UP_BLOCKS = 27
SPAN = 7
PROJECTED, PULLED = 0, 1
FINISH_AT = 3
SPLITS = (2, 2)
FIRST = 3


def hops(offset):
    return sum(min(d, n - d) for d, n in zip(offset, (NX, NL, NY)))


def pick(v, a, b, c, d):
    return jnp.where(v == 0, a, jnp.where(v == 1, b, jnp.where(v == 2, c, d)))


def kernel(
    act, cot, lens, down, up, out,
    data, adapt, lens_s, part, sibling, pair, arrived, tokens, terms, dterms, factors, fishers_in, own, merged, gathered,
    load_sem, small_sem, ex_send, ex_recv, bc_send, bc_recv, tk_send, tk_recv,
    a_send, a_recv, f_send, f_recv, out_send, out_recv, plane_sem, all_sem,
):
    seqs, span, wa = act.shape[1:]
    wc = cot.shape[3]
    rank = down.shape[1]
    half = rank // 2
    c = lax.axis_index("client")
    r = lax.axis_index("row")
    x, lo, y = c // PLANE, (c // NY) % NL, c % NY
    hi, core = r // NCORE, r % NCORE

    def client(dx, dl, dy):
        return lax.rem(x + dx, NX) * PLANE + lax.rem(lo + dl, NL) * NY + lax.rem(y + dy, NY)

    def chip(k):
        return (c, lax.rem(hi + k, NH) * NCORE + core)

    xs = [lax.rem(x + d, NX) * PLANE for d in (2, 1, 3, 0)]
    ls = [lax.rem(lo + d, NL) * NY for d in (1, 0)]
    ys = [lax.rem(y + d, NY) for d in (2, 1, 3, 0)]

    def target(k):
        if isinstance(k, int):
            return xs[k // PLANE] + ls[k % PLANE // NY] + ys[k % NY]
        v, q = k // PLANE, k % PLANE
        return client(pick(v, 2, 1, 3, 0), 1 - q // NY, pick(q % NY, 2, 1, 3, 0))

    def slot_at(to):
        dx, dl, dy = lax.rem(to // PLANE - x + NX, NX), lax.rem(to // NY % NL - lo + NL, NL), lax.rem(to % NY - y + NY, NY)
        return pick(dx, 3, 1, 0, 2) * PLANE + (1 - dl) * NY + pick(dy, 3, 1, 0, 2)

    def rows(unit, n):
        return pl.ds(pl.multiple_of(unit * half, half), n * half)

    def lanes(block):
        return pl.ds(pl.multiple_of(block * LANES, LANES), LANES)

    def is_whole(p, j):
        return j < jnp.where(p < NX - 1, 6, 4)

    def up_block(p, j):
        return jnp.where(p < NX - 1, p * SPAN + jnp.minimum(j, SPAN - 1), jnp.where(j < 4, 21 + j, 25 + (j - 4) // 2))

    def down_block(p, j):
        return jnp.where(p < NX - 1, p, 3 + (j - 4) // 2)

    def first_block(p):
        return jnp.minimum(p * SPAN, UP_BLOCKS - SPAN)

    other = (c, hi * NCORE + 1 - core)
    peers = [other] + [chip(k) for k in (2, 1, 3)]
    along_y = [(client(0, 0, k), r) for k in (2, 1, 3)]
    peers += [(client(k, 0, 0), r) for k in (2, 1, 3)] + along_y + [(client(0, 1, 0), r)]

    small = [
        pltpu.make_async_copy(down.at[0], adapt.at[:, pl.ds(wc, wa)], small_sem.at[0]),
        pltpu.make_async_copy(up.at[0], adapt.at[:, pl.ds(0, wc)], small_sem.at[1]),
        pltpu.make_async_copy(lens, lens_s, small_sem.at[2]),
    ]
    load_act = pltpu.make_async_copy(act.at[0], data.at[:, :, pl.ds(wc, wa)], load_sem.at[seqs])

    def load_cot(e):
        return pltpu.make_async_copy(cot.at[0, e], data.at[e, :, pl.ds(0, wc)], load_sem.at[e])

    loads = [small[0], load_act, small[1]] + [load_cot(e) for e in range(seqs)] + [small[2]]
    for copy in loads[:FIRST]:
        copy.start()

    barrier = pltpu.get_barrier_semaphore()
    for peer in peers:
        pl.semaphore_signal(barrier, inc=1, device_id=peer, device_id_type=MESH)
    for copy in loads[FIRST:]:
        copy.start()

    def remote(src, dst, send, recv, to):
        return pltpu.make_async_remote_copy(
            src_ref=src, dst_ref=dst, send_sem=send, recv_sem=recv, device_id=to, device_id_type=MESH
        )

    ends = [sum(SPLITS[:i + 1]) for i in range(len(SPLITS))]
    steps = 1 + len(SPLITS)

    def piece(step):
        return (PROJECTED, pl.ds(0, seqs)) if step == 0 else (PULLED, pl.ds(ends[step - 1] - SPLITS[step - 1], SPLITS[step - 1]))

    def exchange(step):
        kind, which = piece(step)
        return remote(part.at[kind, 1 - core, which], sibling.at[kind, which], ex_send.at[step], ex_recv.at[step], other)

    def broadcast(step):
        kind, which = piece(step)
        exchange(step).wait_recv()
        pair[kind, which] = (part[kind, core, which] + sibling[kind, which]).astype(BF16)
        for k in (2, 1, 3):
            remote(pair.at[kind, which], arrived.at[kind, k - 1, which], bc_send.at[step], bc_recv.at[step], chip(k)).start()

    def broadcast_all(step):
        kind, which = piece(step)
        ref = arrived.at[kind, :, which]
        return remote(ref, ref, bc_send.at[step], bc_recv.at[step], other)

    def token_swap(kind):
        ref = tokens.at[kind, core]
        return remote(ref, ref, tk_send.at[kind], tk_recv.at[kind], other)

    def finish(kind):
        for step in ((0,) if kind == PROJECTED else range(1, steps)):
            broadcast_all(step).wait_recv()
        position = lax.broadcasted_iota(jnp.int32, (1, span), 1)
        for e in range(seqs):
            total = part[kind, core, e] + sibling[kind, e]
            for k in range(NH - 1):
                total += arrived[kind, k, e].astype(F32)
            length = jnp.full((1, span), lens_s[0, e], jnp.int32)
            weight = (position < length).astype(F32) / length.astype(F32)
            tokens[kind, core, e] = (total * weight).astype(BF16)
        token_swap(kind).start()

    def meet():
        pl.semaphore_wait(barrier, len(peers))
        exchange(0).start()
        for peer in along_y:
            pl.semaphore_signal(plane_sem, inc=1, device_id=peer, device_id_type=MESH)

    load_act.wait()
    small[0].wait()
    for e in range(seqs):
        projected = lax.dot_general(adapt[:, wc:], data[e, :, wc:], NT, preferred_element_type=F32)
        part[PROJECTED, 0, e] = projected[:half]
        part[PROJECTED, 1, e] = projected[half:]
    small[1].wait()

    def pull(e, _):
        load_cot(e).wait()
        pulled = lax.dot_general(adapt[:, :wc], data[e, :, :wc], NT, preferred_element_type=F32)
        part[PULLED, 0, e] = pulled[:half]
        part[PULLED, 1, e] = pulled[half:]

        pl.when(e == 0)(meet)

        for step in range(1, steps):
            pl.when(e == sent_at[step])(exchange(step).start)
        for step in range(steps):
            if cast_at[step] < seqs:
                pl.when(e == cast_at[step])(functools.partial(broadcast, step))
        return 0

    sent_at = [0] + [end - 1 for end in ends]
    cast_at = [0] + [end for end in ends]
    lax.fori_loop(0, seqs, pull, 0)
    for step in range(steps):
        if cast_at[step] >= seqs:
            broadcast(step)
    pl.semaphore_wait(plane_sem, NY - 1)
    pl.semaphore_signal(all_sem, inc=1, device_id=(client(0, 1, 0), r), device_id_type=MESH)
    small[2].wait()

    def give_factors(v, _):
        p = lax.rem(x + pick(v, 2, 1, 3, 0), NX)
        for q in range(PLANE):
            if q < PLANE - 1:
                give_factor(v, p, q)
            else:
                pl.when(v < NX - 1)(functools.partial(give_factor, v, p, q))
        return 0

    def give_factor(v, p, q):
        k = v * PLANE + q
        j = ls[q // NY] + ys[q % NY]
        to = p * PLANE + j
        block, h = up_block(p, j), j % 2

        @pl.when(is_whole(p, j))
        def _():
            remote(adapt.at[:, lanes(block)], factors.at[rows(2 * k, 2)], a_send, a_recv, (to, r)).start()

        @pl.when(jnp.logical_not(is_whole(p, j)))
        def _():
            remote(adapt.at[rows(h, 1), lanes(block)], factors.at[rows(2 * k, 1)], a_send, a_recv, (to, r)).start()
            block2 = wc // LANES + down_block(p, j)
            remote(adapt.at[rows(h, 1), lanes(block2)], factors.at[rows(2 * k + 1, 1)], a_send, a_recv, (to, r)).start()


    pl.semaphore_wait(all_sem, 1)
    lax.fori_loop(0, NX, give_factors, 0)
    finish(PROJECTED)

    def fishers(kind, columns, width):
        total = jnp.zeros((rank, width), F32)
        for e in range(seqs):
            left = jnp.concatenate([tokens[kind, 0, e], tokens[kind, 1, e]], axis=0)
            grad = jnp.dot(left, data[e, :, columns], preferred_element_type=F32)
            total += grad * grad
        return total.astype(BF16)

    token_swap(PROJECTED).wait_recv()

    units = 2 * (wa // LANES)

    def down_stage():
        token_swap(PULLED).wait_recv()
        fisher = fishers(PULLED, pl.ds(wc, wa), wa)
        for b in range(wa // LANES):
            dterms[b * rank:(b + 1) * rank] = fisher[:, b * LANES:(b + 1) * LANES]

        def give_down(k, _):
            n = lax.rem(c + k, units)
            to = jnp.minimum(n // 2, NX - 1) * PLANE + jnp.where(n < 6, 6 + n % 2, n - 2)

            @pl.when(c != to)
            def _():
                remote(dterms.at[rows(n, 1)], fishers_in.at[rows(2 * slot_at(to) + 1, 1)], f_send, f_recv.at[1], (to, r)).start()

            return 0

        lax.fori_loop(0, units, give_down, 0)

    def up_stage(stage, _):
        @pl.when(stage == FINISH_AT)
        def _():
            finish(PULLED)

        p = lax.rem(x + pick(stage, 2, 1, 3, 0), NX)
        first = first_block(p)
        fisher = fishers(PROJECTED, pl.ds(pl.multiple_of(first * LANES, LANES), SPAN * LANES), SPAN * LANES)
        for b in range(SPAN):
            terms[stage, b * rank:(b + 1) * rank] = fisher[:, b * LANES:(b + 1) * LANES]

        def give(q):
            k = stage * PLANE + q
            j = ls[q // NY] + ys[q % NY]
            to = p * PLANE + j
            unit = 2 * (up_block(p, j) - first)

            @pl.when(is_whole(p, j))
            def _():
                remote(terms.at[stage, rows(unit, 2)], fishers_in.at[rows(2 * k, 2)], f_send, f_recv.at[stage // (NX - 1)], (to, r)).start()

            @pl.when(jnp.logical_not(is_whole(p, j)))
            def _():
                remote(terms.at[stage, rows(unit + j % 2, 1)], fishers_in.at[rows(2 * k, 1)], f_send, f_recv.at[stage // (NX - 1)], (to, r)).start()

        for q in range(PLANE):
            if q < PLANE - 1:
                give(q)
            else:
                pl.when(stage < NX - 1)(functools.partial(give, q))
        return 0

    lax.fori_loop(0, NX, up_stage, 0)

    down_stage()

    j = c % PLANE
    whole = is_whole(x, j)
    unit = 2 * (up_block(x, j) - first_block(x))

    @pl.when(whole)
    def _():
        own[0] = terms[NX - 1, rows(unit, 2)]
        own[1] = adapt[:, lanes(up_block(x, j))]

    @pl.when(jnp.logical_not(whole))
    def _():
        block = down_block(x, j)
        own[0, :half] = terms[NX - 1, rows(unit + j % 2, 1)]
        own[0, half:] = dterms[rows(2 * block + j % 2, 1)]
        own[1, :half] = adapt[rows(j % 2, 1), lanes(up_block(x, j))]
        own[1, half:] = adapt[rows(j % 2, 1), lanes(wc // LANES + block)]

    remote(factors, factors, a_send, a_recv, other).wait_recv()
    early = PLANE * (NX - 1)

    def await_units(n, which):
        ref = fishers_in.at[pl.ds(0, n * half)]
        remote(ref, ref, f_send, f_recv.at[which], other).wait_recv()

    def sums(at, start, stop, n):
        total = own[0, at:at + n].astype(F32)
        return add(total, total * own[1, at:at + n].astype(F32), at, start, stop, n)

    def add(total, weighted, at, start, stop, n):
        for k in range(start, stop):
            here = pl.ds(k * rank + at, n)
            fisher = fishers_in[here].astype(F32)
            total += fisher
            weighted += fisher * factors[here].astype(F32)
        return total, weighted

    pl.when(whole)(functools.partial(await_units, 2 * early, 0))
    pl.when(jnp.logical_not(whole))(functools.partial(await_units, early, 0))
    top = sums(0, 0, early, half)
    pl.when(whole)(functools.partial(await_units, 2 * (OWNERS - 1 - early), 1))
    pl.when(jnp.logical_not(whole))(functools.partial(await_units, 2 * (OWNERS - 1) - early, 1))
    top = add(*top, 0, early, OWNERS - 1, half)
    bottom = sums(half, 0, OWNERS - 1, half)
    total, weighted = (jnp.concatenate(pair_of, axis=0) for pair_of in zip(top, bottom))
    merged[...] = (weighted / (total + EPS)).astype(BF16)

    def publish(to):
        remote(merged, gathered.at[rows(2 * c, 2)], out_send, out_recv, (to, r)).start()

    offsets = [(dx, dl, dy) for dx in range(NX) for dl in range(NL) for dy in range(NY)][1:]
    for offset in sorted(offsets, key=lambda o: (-hops(o), (o[0] + o[2]) % 4, o[1])):
        publish(client(*offset))
    gathered[rows(2 * c, 2)] = merged[...]

    for step in range(steps):
        exchange(step).wait_send()
        broadcast_all(step).wait_send()
    for kind in (PROJECTED, PULLED):
        token_swap(kind).wait_send()
    remote(factors, factors, a_send, a_recv, other).wait_send()
    remote(fishers_in, fishers_in, f_send, f_recv.at[0], other).wait_send()
    ref = gathered.at[pl.ds(0, rank * (OWNERS - 1))]
    remote(ref, ref, out_send, out_recv, other).wait()
    for owner in range(OWNERS):
        p, j = owner // PLANE, owner % PLANE
        h = j % 2
        if j < (6 if p < NX - 1 else 4):
            block = SPAN * p + j
            out[:, block * LANES:(block + 1) * LANES] = gathered[owner * rank:(owner + 1) * rank]
        else:
            block, dblock = (SPAN * p + 6, p) if p < NX - 1 else (25 + (j - 4) // 2, 3 + (j - 4) // 2)
            dblock += wc // LANES
            out[h * half:(h + 1) * half, block * LANES:(block + 1) * LANES] = gathered[owner * rank:owner * rank + half]
            out[h * half:(h + 1) * half, dblock * LANES:(dblock + 1) * LANES] = gathered[owner * rank + half:(owner + 1) * rank]


def local(*args):
    activations, cotangent, lengths, adapter_down, adapter_up = args
    _, seqs, span, wa = activations.shape
    wc = cotangent.shape[3]
    rank = adapter_down.shape[1]
    half = rank // 2
    width = wa + wc
    dma = pltpu.SemaphoreType.DMA
    out = pl.pallas_call(
        kernel,
        out_shape=jax.ShapeDtypeStruct((rank, width), BF16),
        in_specs=[pl.BlockSpec(memory_space=pl.ANY)] * 5,
        out_specs=pl.BlockSpec(memory_space=pltpu.VMEM),
        scratch_shapes=[
            pltpu.VMEM((seqs, span, width), BF16),
            pltpu.VMEM((rank, width), BF16),
            pltpu.SMEM((1, seqs), jnp.int32),
            pltpu.VMEM((2, 2, seqs, half, span), F32),
            pltpu.VMEM((2, seqs, half, span), F32),
            pltpu.VMEM((2, seqs, half, span), BF16),
            pltpu.VMEM((2, NH - 1, seqs, half, span), BF16),
            pltpu.VMEM((2, 2, seqs, half, span), BF16),
            pltpu.VMEM((NX, SPAN * rank, LANES), BF16),
            pltpu.VMEM((wa // LANES * rank, LANES), BF16),
            pltpu.VMEM((rank * (OWNERS - 1), LANES), BF16),
            pltpu.VMEM((rank * (OWNERS - 1), LANES), BF16),
            pltpu.VMEM((2, rank, LANES), BF16),
            pltpu.VMEM((rank, LANES), BF16),
            pltpu.VMEM((rank * OWNERS, LANES), BF16),
            dma((seqs + 1,)), dma((3,)), dma((3,)), dma((3,)), dma((3,)), dma((3,)), dma((2,)), dma((2,)),
            dma, dma, dma, dma((2,)), dma, dma, pltpu.SemaphoreType.REGULAR, pltpu.SemaphoreType.REGULAR,
        ],
        compiler_params=pltpu.CompilerParams(
            collective_id=0, has_side_effects=True, vmem_limit_bytes=48 * 1024 * 1024
        ),
    )(*(pltpu.with_memory_space_constraint(a, pltpu.HBM) for a in args))
    return out[:, wc:], out[:, :wc]


def solution(mesh):
    in_specs = (
        P("client", None, None, "row"),
        P("client", None, None, "row"),
        P("client", None),
        P("client", None, "row"),
        P("client", None, "row"),
    )
    out_specs = (P(None, "row"), P(None, "row"))
    return jax.shard_map(local, mesh=mesh, in_specs=in_specs, out_specs=out_specs, check_vma=False)
```
